512 devices in a mesh: lat: 16 (over z), lev: 32 (over x, y, core).
Axes of the slice: x: 4, y: 4, z: 16, core: 2. Of those that a mesh axis runs over, the one named last changes fastest.
Arguments:
- spec_in: bfloat16 [32, 2, 32, 2560], P('lat', None, None, 'lev'), may hold values from -6 to 6
- legendre: bfloat16 [32, 2560, 2560], P('lat', 'lev'), may hold values from -0.125 to 0.125
- pattern: int32 [32, 20, 20], P('lat'), may hold values from 0 to 1, as said below
- deal_list: int32 [32], replicated, may hold values from 0 to 2559, as said below
- circle_lengths: int32 [2560], replicated, may hold values from 12 to 10256, as said below
- mixing: bfloat16 [32, 32], replicated, may hold values from -1 to 1
Outputs:
- spec_out: float32 [32, 2, 32, 2560], P('lat', None, None, 'lev')
The draws below stay inside these ranges and needn't reach their ends.
Inputs may be any that keep to these rules, and one draw needn't show every extreme that they name: `deal_list`: distinct wavenumbers; 0 and 2559 are always among them. pattern[m, a, b] is 1 exactly when b * 128 <= 2559 - deal_list[m] and a >= (deal_list[m] * 20) // 5120, else 0. `circle_lengths`: multiples of 4; row j holds a value between 20 + 4 j - 4 (j // 2 + 2) and 20 + 4 j, and the last row exactly 20 + 4 (2559).
All inputs are finite; a program needn't handle non-finite values.
Results may differ from the reference program's by a relative error of at most 0.0026.
Values may be sent and summed in bfloat16 or wider, within the bound.
No kernel may reach another device: no remote copies, remote signals or barrier semaphores. Data moves between devices by JAX's collectives and lax.ppermute only.
A program may use at most 64 MiB of HBM per device.

```python
import math
import jax
import jax.numpy as jnp
from jax import lax

NLAT = 5120
NK = 2560
BLK = 128
HLAT = 2560
MW = 32
FIELDS = 32


def common_waves(key):
    first_key = jax.random.fold_in(key, 11)
    second_key = jax.random.fold_in(key, 12)
    middle = 1 + jax.random.permutation(first_key, NK - 2)[:MW - 2]
    chosen = jnp.concatenate([jnp.array([0, NK - 1], dtype=jnp.int32), middle.astype(jnp.int32)])
    return jax.random.permutation(second_key, chosen)


def draw_deal_list(key, part):
    return common_waves(key)


def draw_pattern(key, part):
    wavenums = common_waves(key)
    row_blocks = jnp.arange(HLAT // BLK, dtype=jnp.int32)
    col_blocks = jnp.arange(NK // BLK, dtype=jnp.int32)
    polar_cut = wavenums * (HLAT // BLK) // (2 * NK)
    rows_live = row_blocks[None, :] >= polar_cut[:, None]
    cols_live = col_blocks[None, :] * BLK <= (NK - 1 - wavenums)[:, None]
    return (rows_live[:, :, None] & cols_live[:, None, :]).astype(jnp.int32)


def draw_circle_lengths(key, part):
    row_ids = jnp.arange(HLAT, dtype=jnp.int32)
    upper = (row_ids // 2 + 3).astype(jnp.int32)
    dropped = jax.random.randint(jax.random.fold_in(key, 21), (HLAT,), 0, upper).astype(jnp.int32)
    dropped = jnp.where(row_ids == HLAT - 1, 0, dropped)
    return (20 + 4 * row_ids - 4 * dropped).astype(jnp.int32)


def steps_of(stream_key, shape, split, smallest, largest):
    loudness, own = 1.0, jax.random.fold_in(stream_key, 6)
    for dim, shards_of in split:
        heights = jnp.exp(jax.random.uniform(jax.random.fold_in(own, dim), (shards_of,), jnp.float32, smallest / len(split), largest / len(split)))
        loudness = loudness * jnp.repeat(heights, shape[dim] // shards_of).reshape([-1 if axis == dim else 1 for axis in range(len(shape))])
    return loudness


def normal_values(own_key, dims, spread, most, shards=(), kind=jnp.bfloat16):
    values = jax.random.normal(own_key, dims, jnp.float32) * spread
    if len(shards) > 0:
        values = steps_of(own_key, dims, shards, -0.22, 0.18) * values
    return jnp.clip(values, min=-most, max=most).astype(kind)


def setup_inputs(seed: int = 0) -> dict:
    seeds = jax.random.split(jax.random.key(seed), 7)
    spec_in = normal_values(seeds[0], (MW, 2, FIELDS, NK), 1.0, 6.0, ((0, 16), (3, 32)))
    legendre = normal_values(seeds[1], (MW, NK, HLAT), NK ** -0.5, 0.125, ((0, 16), (1, 32)))
    pattern = draw_pattern(jax.random.fold_in(seeds[6], 71), 0)
    deal_list = draw_deal_list(jax.random.fold_in(seeds[6], 71), 0)
    circle_lengths = draw_circle_lengths(jax.random.fold_in(seeds[6], 71), 0)
    mixing = normal_values(seeds[5], (FIELDS, FIELDS), FIELDS ** -0.5, 1.0)
    return {"spec_in": spec_in, "legendre": legendre, "pattern": pattern, "deal_list": deal_list, "circle_lengths": circle_lengths, "mixing": mixing}


def live_table(block_mask, dense_rows):
    expanded = jnp.repeat(jnp.repeat(block_mask, BLK, axis=0), BLK, axis=1)
    return dense_rows.astype(jnp.float32) * jnp.transpose(expanded).astype(jnp.float32)

def circle_tables(wavenums, length):
    lon_count = 20 + 4 * (HLAT - 1)
    positions = jnp.arange(lon_count, dtype=jnp.int32)
    phases = wavenums.astype(jnp.int32)[:, None] * positions[None, :] % length
    angles = phases.astype(jnp.float32) * (2.0 * math.pi) / length.astype(jnp.float32)
    inside = positions[None, :] < length
    cosine_table = jnp.where(inside, jnp.cos(angles), 0.0).astype(jnp.bfloat16)
    sine_table = jnp.where(inside, jnp.sin(angles), 0.0).astype(jnp.bfloat16)
    return (cosine_table, sine_table)

def reference(spec_in, legendre, pattern, deal_list, circle_lengths, mixing):
    parity = (1 - 2 * (jnp.arange(NK, dtype=jnp.int32) % 2)).astype(jnp.float32)

    def inverse_one(inputs):
        dense_rows, block_mask, coeffs = inputs
        masked = live_table(block_mask, dense_rows)
        coeff_f = coeffs.astype(jnp.float32)
        stacked = jnp.stack([coeff_f, coeff_f * parity], axis=0)
        return jnp.einsum('kj,hrfk->hrfj', masked, stacked).astype(jnp.bfloat16)
    fourier = lax.map(inverse_one, (legendre, pattern, spec_in))
    rows_first = jnp.moveaxis(fourier, 4, 0)
    mixing_f = mixing.astype(jnp.float32)
    synth_scale = (2.0 * MW) ** (-0.5)

    def row_one(inputs):
        fourier_row, row_id = inputs
        length = circle_lengths[row_id]
        cosine_table, sine_table = circle_tables(deal_list, length)
        phases_table = jnp.concatenate([cosine_table, -sine_table], axis=0).astype(jnp.float32)
        coeffs = jnp.transpose(fourier_row, (1, 3, 2, 0)).reshape(2 * FIELDS, 2 * MW).astype(jnp.float32)
        grid_values = (jnp.dot(coeffs, phases_table) * synth_scale).astype(jnp.bfloat16)
        grid_f = grid_values.astype(jnp.float32).reshape(2, FIELDS, -1)
        mixed_sum = jnp.einsum('fg,hgl->hfl', mixing_f, grid_f)
        column = (grid_f + jnp.tanh(mixed_sum)).astype(jnp.bfloat16).reshape(2 * FIELDS, -1)
        weight = jnp.sin(math.pi * (row_id.astype(jnp.float32) + 0.5) / NLAT) / jnp.sqrt(length.astype(jnp.float32))
        analysis = (jnp.dot(column.astype(jnp.float32), phases_table.T) * weight).astype(jnp.bfloat16)
        return jnp.transpose(analysis.reshape(2, FIELDS, 2, MW), (3, 0, 2, 1))
    analysed = lax.map(row_one, (rows_first, jnp.arange(HLAT, dtype=jnp.int32)))
    analysed = jnp.moveaxis(analysed, 0, 4)

    def direct_one(inputs):
        dense_rows, block_mask, coeffs = inputs
        masked = live_table(block_mask, dense_rows)
        product = jnp.einsum('kj,hrfj->hrfk', masked, coeffs.astype(jnp.float32))
        return product[0] + parity * product[1]
    return lax.map(direct_one, (legendre, pattern, analysed))
```

```python
import math

import jax
import jax.numpy as jnp
from jax import lax
from jax.experimental import pallas as pl
from jax.experimental.pallas import tpu as pltpu
from jax.sharding import PartitionSpec as P

BLK = 128
F32 = jnp.float32
BF16 = jnp.bfloat16
VMEM = pl.BlockSpec(memory_space=pltpu.VMEM)
SMEM = pl.BlockSpec(memory_space=pltpu.SMEM)
NT = (((1,), (1,)), ((), ()))


def params(mib):
    return pltpu.CompilerParams(vmem_limit_bytes=mib * 1024 * 1024)


def block_mask(pattern_ref, slot, row_block, first_col, shape):
    cols = shape[0]
    low = first_col // BLK
    high = (first_col + cols - 1) // BLK
    inner = lax.broadcasted_iota(jnp.int32, shape, 0) + first_col
    return jnp.where(
        inner < (low + 1) * BLK,
        pattern_ref[slot, row_block, low],
        pattern_ref[slot, row_block, high],
    ).astype(F32).astype(BF16)


def masked_half(leg_ref, pattern_ref, slot, fifth, core, first_col):
    parts = []
    cols = leg_ref.shape[1]
    for half in range(2):
        row_block = 4 * fifth + 2 * core + half
        start = pl.multiple_of(row_block * BLK, BLK)
        values = leg_ref[slot, :, pl.ds(start, BLK)]
        parts.append(values * block_mask(pattern_ref, slot, row_block, first_col, (cols, BLK)))
    return jnp.concatenate(parts, axis=1)


def inverse_kernel(place_ref, pattern_ref, spec_ref, other_spec_ref, leg_ref, other_leg_ref, out_ref):
    lev = place_ref[1]
    core = lax.rem(lev, 2)
    slots, _, fields, cols = spec_ref.shape
    chips = out_ref.shape[0]
    fifths = out_ref.shape[1] // (16 * slots)

    def stacked(ref, slot, first_col):
        column = lax.broadcasted_iota(jnp.int32, (fields, cols), 1) + first_col
        parity = (1 - 2 * lax.rem(column, 2)).astype(F32)
        rows = []
        for part in range(2):
            values = ref[slot, part].astype(F32)
            rows.append(values.astype(BF16))
            rows.append((values * parity).astype(BF16))
        return jnp.concatenate(rows, axis=0)

    mine = lev * cols
    theirs = (lev + 1 - 2 * core) * cols
    for slot in range(slots):
        left = stacked(spec_ref, slot, mine)
        other_left = stacked(other_spec_ref, slot, theirs)
        for fifth in range(fifths):
            right = masked_half(leg_ref, pattern_ref, slot, fifth, core, mine)
            other_right = masked_half(other_leg_ref, pattern_ref, slot, fifth, core, theirs)
            value = jnp.dot(left, right, preferred_element_type=F32)
            value = value + jnp.dot(other_left, other_right, preferred_element_type=F32)
            start = (slot * fifths + fifth) * 16
            out_ref[:, start : start + 16, :] = value.T.astype(BF16).reshape(chips, 16, BLK)


def sum_kernel(in_ref, out_ref, spread):
    chips, rows, _ = in_ref.shape
    lats = out_ref.shape[0]
    groups = rows // 16
    fifths = groups // 2
    spread[...] = jnp.zeros_like(spread)
    for group in range(groups):
        piece = slice(group * 16, group * 16 + 16)
        total = in_ref[0, piece, :].astype(F32)
        for chip in range(1, chips):
            total = total + in_ref[chip, piece, :].astype(F32)
        slot, fifth = divmod(group, fifths)
        spread[pl.ds(slot * 8 + fifth, lats, stride=16), :] = total
    out_ref[...] = spread[...].astype(BF16).reshape(out_ref.shape)


def copies_kernel(in_ref, out_ref, spread):
    chips, rows, _ = out_ref.shape
    lats = in_ref.shape[0]
    groups = rows // 16
    fifths = groups // 2
    spread[...] = in_ref[...].astype(F32).reshape(spread.shape)
    for group in range(groups):
        slot, fifth = divmod(group, fifths)
        value = spread[pl.ds(slot * 8 + fifth, lats, stride=16), :].astype(BF16)
        for chip in range(chips):
            out_ref[chip, group * 16 : group * 16 + 16, :] = value


def circle(x, length):
    quarter = length * 0.25
    per = 1.0 / quarter
    turns = jnp.floor(x * per + 0.5)
    rest = x - turns * quarter
    more = jnp.floor(rest * per + 0.5)
    rest = rest - more * quarter
    turns = turns + more
    turns = turns - 4.0 * jnp.floor(turns * 0.25)
    angle = rest * ((2.0 * math.pi) / length)
    sq = angle * angle
    sine = angle * (
        1.0 + sq * (-1.0 / 6 + sq * (1.0 / 120 + sq * (-1.0 / 5040 + sq * (1.0 / 362880))))
    )
    cosine = 1.0 + sq * (
        -0.5 + sq * (1.0 / 24 + sq * (-1.0 / 720 + sq * (1.0 / 40320 + sq * (-1.0 / 3628800))))
    )
    odd = (turns == 1.0) | (turns == 3.0)
    first = jnp.where(odd, sine, cosine)
    second = jnp.where(odd, cosine, sine)
    first = jnp.where((turns == 1.0) | (turns == 2.0), -first, first)
    second = jnp.where(turns >= 2.0, -second, second)
    return first, second


def row_of(place_ref, fifth, lats, chips):
    lat, lev = place_ref[0], place_ref[1]
    return fifth * (2 * lats * chips) + lax.rem(lev, 2) * (lats * chips) + (lev // 2) * lats + lat


def table_kernel(sizes, lats, chips, half_lat, place_ref, deal_ref, lengths_ref, mixing_ref,
                 table_ref, turn_ref, weight_ref, mix_ref):
    waves = deal_ref.shape[0]
    fields = mixing_ref.shape[0]
    shape = (waves, BLK)
    sub = lax.broadcasted_iota(jnp.int32, shape, 0)
    lane = lax.broadcasted_iota(jnp.int32, shape, 1)
    lane_f = lane.astype(F32)
    wave = jnp.zeros(shape, jnp.int32)
    for slot in range(waves):
        wave = jnp.where(sub == slot, deal_ref[slot], wave)
    wave_f = wave.astype(F32)
    for pair in range(2):
        quarter = 2 * pair + (lane >= BLK // 2).astype(jnp.int32)
        turn = lax.rem(quarter * wave, 4)
        turn_ref[2 * pair] = jnp.where(turn == 0, 1.0, jnp.where(turn == 2, -1.0, 0.0))
        turn_ref[2 * pair + 1] = jnp.where(turn == 1, 1.0, jnp.where(turn == 3, -1.0, 0.0))
    size = mix_ref.shape[0]
    pick = (
        lax.rem(lax.broadcasted_iota(jnp.int32, (size, fields), 0), fields)
        == lax.broadcasted_iota(jnp.int32, (size, fields), 1)
    ).astype(F32).astype(BF16)
    tall = jnp.dot(pick, mixing_ref[...], preferred_element_type=F32).astype(BF16)
    wide = lax.dot_general(tall, pick, NT, preferred_element_type=F32)
    same = (
        lax.broadcasted_iota(jnp.int32, (size, size), 0) // fields
        == lax.broadcasted_iota(jnp.int32, (size, size), 1) // fields
    )
    mix_ref[...] = jnp.where(same, wide, 0.0).astype(BF16)
    weight_ref[...] = jnp.zeros_like(weight_ref)
    start = 0
    for fifth, blocks in enumerate(sizes):
        row = row_of(place_ref, fifth, lats, chips)
        length = lengths_ref[row]
        points = length // 4
        length_f = jnp.full(shape, length, jnp.int32).astype(F32)
        low_cos, low_sin = circle(wave_f * lane_f, length_f)
        high_cos, high_sin = circle(wave_f * lane_f * float(BLK), length_f)
        for block in range(blocks):
            a_cos = jnp.broadcast_to(high_cos[:, block : block + 1], shape)
            a_sin = jnp.broadcast_to(high_sin[:, block : block + 1], shape)
            cosine = a_cos * low_cos - a_sin * low_sin
            sine = a_sin * low_cos + a_cos * low_sin
            inside = lane + block * BLK < points
            here = slice((start + block) * BLK, (start + block + 1) * BLK)
            table_ref[0:waves, here] = jnp.where(inside, cosine, 0.0).astype(BF16)
            table_ref[waves : 2 * waves, here] = jnp.where(inside, -sine, 0.0).astype(BF16)
        start += blocks
        one = (1, BLK)
        row_f = jnp.full(one, row, jnp.int32).astype(F32) + 0.5
        _, sine = circle(row_f, jnp.full(one, 4.0 * half_lat, F32))
        weight_ref[fifth : fifth + 1, :] = sine / jnp.sqrt(length_f[0:1, :])


def grid_kernel(sizes, scale, in_ref, table_ref, turn_ref, weight_ref, mix_ref, out_ref, spread, gathered):
    waves = turn_ref.shape[1]
    lane = lax.broadcasted_iota(jnp.int32, (waves, BLK), 1)
    front = lane < BLK // 2
    spread[...] = in_ref[...].astype(F32).reshape(spread.shape)
    gathered[...] = jnp.zeros_like(gathered)
    mix = mix_ref[...]
    start = 0
    for fifth, blocks in enumerate(sizes):
        value = spread[pl.ds(fifth, waves, stride=8), :] * scale
        swapped = pltpu.roll(value, BLK // 2, axis=1)
        real = jnp.where(front, value, swapped)
        imag = jnp.where(front, swapped, value)
        tops, bottoms = [], []
        for pair in range(2):
            cosine, sine = turn_ref[2 * pair], turn_ref[2 * pair + 1]
            tops.append(cosine * real - sine * imag)
            bottoms.append(sine * real + cosine * imag)
        coeffs = jnp.concatenate(
            [jnp.concatenate(tops, axis=1), jnp.concatenate(bottoms, axis=1)], axis=0
        ).T.astype(BF16)

        total = jnp.zeros((2 * waves, 2 * BLK), F32)
        done = 0
        while done < blocks:
            take = min(4, blocks - done)
            here = slice((start + done) * BLK, (start + done + take) * BLK)
            table = table_ref[:, here]
            grid = jnp.dot(coeffs, table, preferred_element_type=F32).astype(BF16)
            mixed = jnp.dot(mix, grid, preferred_element_type=F32)
            column = (grid.astype(F32) + jnp.tanh(mixed)).astype(BF16)
            total = total + lax.dot_general(table, column, NT, preferred_element_type=F32)
            done += take
        start += blocks

        real_sum = jnp.zeros((waves, BLK), F32)
        imag_sum = jnp.zeros((waves, BLK), F32)
        for pair in range(2):
            cosine, sine = turn_ref[2 * pair], turn_ref[2 * pair + 1]
            lanes = slice(pair * BLK, (pair + 1) * BLK)
            with_cos, with_sin = total[0:waves, lanes], total[waves : 2 * waves, lanes]
            real_sum = real_sum + cosine * with_cos + sine * with_sin
            imag_sum = imag_sum + cosine * with_sin - sine * with_cos
        real_sum = real_sum + pltpu.roll(real_sum, BLK // 2, axis=1)
        imag_sum = imag_sum + pltpu.roll(imag_sum, BLK // 2, axis=1)
        result = jnp.where(front, real_sum, imag_sum) * weight_ref[fifth : fifth + 1, :]
        gathered[pl.ds(fifth, waves, stride=8), :] = result
    out_ref[...] = gathered[...].astype(BF16).reshape(out_ref.shape)


def direct_kernel(place_ref, pattern_ref, mine_ref, other_ref, leg_ref, out_ref):
    lev = place_ref[1]
    core = lax.rem(lev, 2)
    slots, cols, _ = leg_ref.shape
    fields = out_ref.shape[2]
    chips, rows, _ = mine_ref.shape
    fifths = rows // (16 * slots)
    first = lev * cols
    degree = lax.broadcasted_iota(jnp.int32, (cols, BLK), 0) + first
    parity = (1 - 2 * lax.rem(degree, 2)).astype(F32)
    for slot in range(slots):
        total = jnp.zeros((cols, BLK), F32)
        for fifth in range(fifths):
            start = (slot * fifths + fifth) * 16
            for ref, owner in ((mine_ref, core), (other_ref, 1 - core)):
                left = masked_half(leg_ref, pattern_ref, slot, fifth, owner, first)
                right = ref[:, start : start + 16, :].reshape(chips * 16, BLK)
                total = total + jnp.dot(left, right, preferred_element_type=F32)
        total = total + parity * pltpu.roll(total, BLK - fields, axis=1)
        turned = total.T
        for part in range(2):
            out_ref[slot, part] = turned[2 * part * fields : (2 * part + 1) * fields, :]


def local(spec_in, legendre, pattern, deal_list, circle_lengths, mixing):
    lats, levs = lax.axis_size("lat"), lax.axis_size("lev")
    chips = levs // 2
    slots, cols, half_lat = legendre.shape
    fields = spec_in.shape[2]
    waves = deal_list.shape[0]
    fifths = half_lat // (lats * levs)
    sizes = [
        -(-(5 + (half_lat // fifths) * (fifth + 1) - 1) // BLK) for fifth in range(fifths)
    ]
    place = jnp.stack([lax.axis_index("lat"), lax.axis_index("lev")]).astype(jnp.int32)
    pairs = [(lev, lev ^ 1) for lev in range(levs)]
    same_core = [[2 * chip + core for chip in range(chips)] for core in range(2)]
    rows = slots * fifths * 16

    other_leg = lax.ppermute(legendre, "lev", pairs)
    other_spec = lax.ppermute(spec_in, "lev", pairs)

    table, turns, weights, mix = pl.pallas_call(
        lambda *refs: table_kernel(sizes, lats, chips, half_lat, *refs),
        out_shape=(
            jax.ShapeDtypeStruct((2 * waves, sum(sizes) * BLK), BF16),
            jax.ShapeDtypeStruct((4, waves, BLK), F32),
            jax.ShapeDtypeStruct((8, BLK), F32),
            jax.ShapeDtypeStruct((8 * fields, 8 * fields), BF16),
        ),
        in_specs=[SMEM, SMEM, SMEM, VMEM],
        out_specs=(VMEM, VMEM, VMEM, VMEM),
        compiler_params=params(16),
        cost_estimate=pl.CostEstimate(flops=20_000_000, bytes_accessed=4_000_000, transcendentals=0),
        name="tables",
    )(place, deal_list, circle_lengths, mixing)

    partial_sums = pl.pallas_call(
        inverse_kernel,
        out_shape=jax.ShapeDtypeStruct((chips, rows, BLK), BF16),
        in_specs=[SMEM, SMEM, VMEM, VMEM, VMEM, VMEM],
        out_specs=VMEM,
        compiler_params=params(16),
        name="inverse",
    )(place, pattern, spec_in, other_spec, legendre, other_leg)
    parts = lax.all_to_all(
        partial_sums, "lev", 0, 0, tiled=True, axis_index_groups=same_core
    )
    fourier = pl.pallas_call(
        sum_kernel,
        out_shape=jax.ShapeDtypeStruct((lats, 16, BLK), BF16),
        in_specs=[VMEM],
        out_specs=VMEM,
        scratch_shapes=[pltpu.VMEM((lats * 16, BLK), F32)],
        compiler_params=params(16),
        name="sums",
    )(parts)
    fourier = lax.all_to_all(fourier, "lat", 0, 0, tiled=True)
    analysed = pl.pallas_call(
        lambda *refs: grid_kernel(sizes, (2.0 * waves) ** (-0.5), *refs),
        out_shape=jax.ShapeDtypeStruct((lats, 16, BLK), BF16),
        in_specs=[VMEM] * 5,
        out_specs=VMEM,
        scratch_shapes=[pltpu.VMEM((lats * 16, BLK), F32), pltpu.VMEM((lats * 16, BLK), F32)],
        compiler_params=params(24),
        name="grid_rows",
    )(fourier, table, turns, weights, mix)
    analysed = lax.all_to_all(analysed, "lat", 0, 0, tiled=True)
    copies = pl.pallas_call(
        copies_kernel,
        out_shape=jax.ShapeDtypeStruct((chips, rows, BLK), BF16),
        in_specs=[VMEM],
        out_specs=VMEM,
        scratch_shapes=[pltpu.VMEM((lats * 16, BLK), F32)],
        compiler_params=params(16),
        name="copies",
    )(analysed)
    mine = lax.all_to_all(copies, "lev", 0, 0, tiled=True, axis_index_groups=same_core)
    other = lax.ppermute(mine, "lev", pairs)
    return pl.pallas_call(
        direct_kernel,
        out_shape=jax.ShapeDtypeStruct((slots, 2, fields, cols), F32),
        in_specs=[SMEM, SMEM, VMEM, VMEM, VMEM],
        out_specs=VMEM,
        compiler_params=params(16),
        name="direct",
    )(place, pattern, mine, other, legendre)


def solution(mesh):
    return jax.shard_map(
        local,
        mesh=mesh,
        in_specs=(
            P("lat", None, None, "lev"),
            P("lat", "lev", None),
            P("lat", None, None),
            P(),
            P(),
            P(),
        ),
        out_specs=P("lat", None, None, "lev"),
        check_vma=False,
    )
```

```python
import math

import jax
import jax.numpy as jnp
from jax import lax
from jax.experimental import pallas as pl
from jax.experimental.pallas import tpu as pltpu
from jax.sharding import PartitionSpec as P

BLK = 128
DEGREES = 2560
F32 = jnp.float32
BF16 = jnp.bfloat16
VMEM = pl.BlockSpec(memory_space=pltpu.VMEM)
ANY = pl.BlockSpec(memory_space=pl.ANY)
SMEM = pl.BlockSpec(memory_space=pltpu.SMEM)
NT = (((1,), (1,)), ((), ()))


def params(mib):
    return pltpu.CompilerParams(vmem_limit_bytes=mib * 1024 * 1024)


def live_degrees(wave, first_col, shape):
    degree = lax.broadcasted_iota(jnp.int32, shape, 0) + first_col
    return degree // BLK * BLK <= DEGREES - 1 - wave


def mask_rows(value, wave, degrees_live, row_block, row_blocks):
    rows_live = row_block >= wave * row_blocks // (2 * DEGREES)
    flags = jnp.logical_and(degrees_live, rows_live)
    return jnp.where(flags, value, jnp.zeros_like(value))


def pack_kernel(place_ref, spec_ref, leg_ref, out_ref, spec_vmem, sems):
    other = 1 - lax.rem(place_ref[1], 2)
    slots, cols, half_lat = leg_ref.shape
    fields = spec_ref.shape[2]
    fifths = half_lat // 512
    copies = [pltpu.make_async_copy(spec_ref, spec_vmem, sems.at[0])]
    for slot in range(slots):
        for block in range(2 * fifths):
            fifth, half = divmod(block, 2)
            start = pl.multiple_of((4 * fifth + 2 * other + half) * BLK, BLK)
            begin = (slot * 2 * fifths + block) * cols
            copies.append(
                pltpu.make_async_copy(
                    leg_ref.at[slot, :, pl.ds(start, BLK)],
                    out_ref.at[begin : begin + cols, :],
                    sems.at[len(copies)],
                )
            )
    for copy in copies:
        copy.start()
    begin = slots * 2 * fifths * cols
    out_ref[begin:, :] = jnp.zeros((slots * 2 * fields, BLK), BF16)
    copies[0].wait()
    for slot in range(slots):
        for part in range(2):
            out_ref[begin : begin + fields, 0:cols] = spec_vmem[slot, part]
            begin += fields
    for copy in copies[1:]:
        copy.wait()


def inverse_kernel(place_ref, deal_ref, spec_ref, own_ref, packed_ref, out_ref, other_ref):
    lat, lev = place_ref[0], place_ref[1]
    core = lax.rem(lev, 2)
    slots, _, fields, cols = spec_ref.shape
    chips = out_ref.shape[0]
    fifths = out_ref.shape[1] // (16 * slots)
    mine = lev * cols
    theirs = (lev + 1 - 2 * core) * cols

    def stacked(pieces, first_col):
        column = lax.broadcasted_iota(jnp.int32, (fields, cols), 1) + first_col
        parity = (1 - 2 * lax.rem(column, 2)).astype(F32)
        rows = []
        for piece in pieces:
            rows.append(piece)
            rows.append((piece.astype(F32) * parity).astype(BF16))
        return jnp.concatenate(rows, axis=0)

    spec_start = slots * 2 * fifths * cols
    for slot in range(slots):
        wave = deal_ref[slots * lat + slot]
        live = live_degrees(wave, theirs, (cols, BLK))
        left = stacked([spec_ref[slot, part] for part in range(2)], mine)
        begin = spec_start + slot * 2 * fields
        other_left = stacked(
            [
                packed_ref[begin + part * fields : begin + (part + 1) * fields, 0:cols]
                for part in range(2)
            ],
            theirs,
        )
        for fifth in range(fifths):
            parts = []
            for half in range(2):
                begin = (slot * 2 * fifths + 2 * fifth + half) * cols
                value = packed_ref[begin : begin + cols, :]
                row_block = 4 * fifth + 2 * core + half
                parts.append(mask_rows(value, wave, live, row_block, 4 * fifths))
            other_right = jnp.concatenate(parts, axis=1)
            here = slice(fifth * 2 * BLK, (fifth + 1) * 2 * BLK)
            other_ref[slot, :, here] = other_right
            value = jnp.dot(left, own_ref[slot, :, here], preferred_element_type=F32)
            value = value + jnp.dot(other_left, other_right, preferred_element_type=F32)
            start = (slot * fifths + fifth) * 16
            out_ref[:, start : start + 16, :] = value.T.astype(BF16).reshape(chips, 16, BLK)


def sum_kernel(in_ref, out_ref, spread):
    chips, rows, _ = in_ref.shape
    lats = out_ref.shape[0]
    groups = rows // 16
    fifths = groups // 2
    spread[...] = jnp.zeros_like(spread)
    for group in range(groups):
        piece = slice(group * 16, group * 16 + 16)
        total = in_ref[0, piece, :].astype(F32)
        for chip in range(1, chips):
            total = total + in_ref[chip, piece, :].astype(F32)
        slot, fifth = divmod(group, fifths)
        spread[pl.ds(slot * 8 + fifth, lats, stride=16), :] = total
    out_ref[...] = spread[...].astype(BF16).reshape(out_ref.shape)


def copies_kernel(in_ref, out_ref, spread):
    chips, rows, _ = out_ref.shape
    lats = in_ref.shape[0]
    groups = rows // 16
    fifths = groups // 2
    spread[...] = in_ref[...].astype(F32).reshape(spread.shape)
    for group in range(groups):
        slot, fifth = divmod(group, fifths)
        value = spread[pl.ds(slot * 8 + fifth, lats, stride=16), :].astype(BF16)
        for chip in range(chips):
            out_ref[chip, group * 16 : group * 16 + 16, :] = value


def circle(x, length):
    quarter = length * 0.25
    per = 1.0 / quarter
    turns = jnp.floor(x * per + 0.5)
    rest = x - turns * quarter
    more = jnp.floor(rest * per + 0.5)
    rest = rest - more * quarter
    turns = turns + more
    turns = turns - 4.0 * jnp.floor(turns * 0.25)
    angle = rest * ((2.0 * math.pi) / length)
    sq = angle * angle
    sine = angle * (
        1.0 + sq * (-1.0 / 6 + sq * (1.0 / 120 + sq * (-1.0 / 5040 + sq * (1.0 / 362880))))
    )
    cosine = 1.0 + sq * (
        -0.5 + sq * (1.0 / 24 + sq * (-1.0 / 720 + sq * (1.0 / 40320 + sq * (-1.0 / 3628800))))
    )
    odd = (turns == 1.0) | (turns == 3.0)
    first = jnp.where(odd, sine, cosine)
    second = jnp.where(odd, cosine, sine)
    first = jnp.where((turns == 1.0) | (turns == 2.0), -first, first)
    second = jnp.where(turns >= 2.0, -second, second)
    return first, second


def row_of(place_ref, fifth, lats, chips):
    lat, lev = place_ref[0], place_ref[1]
    return fifth * (2 * lats * chips) + lax.rem(lev, 2) * (lats * chips) + (lev // 2) * lats + lat


def table_kernel(sizes, lats, chips, half_lat, place_ref, deal_ref, lengths_ref, mixing_ref, leg_ref,
                 table_ref, turn_ref, weight_ref, mix_ref, own_ref, sems):
    core = lax.rem(place_ref[1], 2)
    slots, cols, _ = leg_ref.shape
    copies = []
    for slot in range(slots):
        for fifth in range(len(sizes)):
            begin = pl.multiple_of((2 * fifth + core) * 2 * BLK, 2 * BLK)
            copies.append(
                pltpu.make_async_copy(
                    leg_ref.at[slot, :, pl.ds(begin, 2 * BLK)],
                    own_ref.at[slot, :, fifth * 2 * BLK : (fifth + 1) * 2 * BLK],
                    sems.at[len(copies)],
                )
            )
            copies[-1].start()
    waves = deal_ref.shape[0]
    fields = mixing_ref.shape[0]
    shape = (waves, BLK)
    sub = lax.broadcasted_iota(jnp.int32, shape, 0)
    lane = lax.broadcasted_iota(jnp.int32, shape, 1)
    lane_f = lane.astype(F32)
    wave = jnp.zeros(shape, jnp.int32)
    for slot in range(waves):
        wave = jnp.where(sub == slot, deal_ref[slot], wave)
    wave_f = wave.astype(F32)
    for pair in range(2):
        quarter = 2 * pair + (lane >= BLK // 2).astype(jnp.int32)
        turn = lax.rem(quarter * wave, 4)
        turn_ref[2 * pair] = jnp.where(turn == 0, 1.0, jnp.where(turn == 2, -1.0, 0.0))
        turn_ref[2 * pair + 1] = jnp.where(turn == 1, 1.0, jnp.where(turn == 3, -1.0, 0.0))
    size = mix_ref.shape[0]
    pick = (
        lax.rem(lax.broadcasted_iota(jnp.int32, (size, fields), 0), fields)
        == lax.broadcasted_iota(jnp.int32, (size, fields), 1)
    ).astype(F32).astype(BF16)
    tall = jnp.dot(pick, mixing_ref[...], preferred_element_type=F32).astype(BF16)
    wide = lax.dot_general(tall, pick, NT, preferred_element_type=F32)
    same = (
        lax.broadcasted_iota(jnp.int32, (size, size), 0) // fields
        == lax.broadcasted_iota(jnp.int32, (size, size), 1) // fields
    )
    mix_ref[...] = jnp.where(same, wide, 0.0).astype(BF16)
    weight_ref[...] = jnp.zeros_like(weight_ref)
    start = 0
    for fifth, blocks in enumerate(sizes):
        row = row_of(place_ref, fifth, lats, chips)
        length = lengths_ref[row]
        points = length // 4
        length_f = jnp.full(shape, length, jnp.int32).astype(F32)
        low_cos, low_sin = circle(wave_f * lane_f, length_f)
        high_cos, high_sin = circle(wave_f * lane_f * float(BLK), length_f)
        for block in range(blocks):
            a_cos = jnp.broadcast_to(high_cos[:, block : block + 1], shape)
            a_sin = jnp.broadcast_to(high_sin[:, block : block + 1], shape)
            cosine = a_cos * low_cos - a_sin * low_sin
            sine = a_sin * low_cos + a_cos * low_sin
            inside = lane + block * BLK < points
            here = slice((start + block) * BLK, (start + block + 1) * BLK)
            table_ref[0:waves, here] = jnp.where(inside, cosine, 0.0).astype(BF16)
            table_ref[waves : 2 * waves, here] = jnp.where(inside, -sine, 0.0).astype(BF16)
        start += blocks
        one = (1, BLK)
        row_f = jnp.full(one, row, jnp.int32).astype(F32) + 0.5
        _, sine = circle(row_f, jnp.full(one, 4.0 * half_lat, F32))
        weight_ref[fifth : fifth + 1, :] = sine / jnp.sqrt(length_f[0:1, :])
    for copy in copies:
        copy.wait()
    for slot in range(slots):
        number = deal_ref[slots * place_ref[0] + slot]
        live = live_degrees(number, place_ref[1] * cols, (cols, BLK))
        for fifth in range(len(sizes)):
            for half in range(2):
                here = slice((2 * fifth + half) * BLK, (2 * fifth + half + 1) * BLK)
                row_block = 4 * fifth + 2 * core + half
                own_ref[slot, :, here] = mask_rows(
                    own_ref[slot, :, here], number, live, row_block, 4 * len(sizes)
                )


def grid_kernel(sizes, scale, in_ref, table_ref, turn_ref, weight_ref, mix_ref, out_ref, spread, gathered):
    waves = turn_ref.shape[1]
    lane = lax.broadcasted_iota(jnp.int32, (waves, BLK), 1)
    front = lane < BLK // 2
    spread[...] = in_ref[...].astype(F32).reshape(spread.shape)
    gathered[...] = jnp.zeros_like(gathered)
    mix = mix_ref[...]
    start = 0
    for fifth, blocks in enumerate(sizes):
        value = spread[pl.ds(fifth, waves, stride=8), :] * scale
        swapped = pltpu.roll(value, BLK // 2, axis=1)
        real = jnp.where(front, value, swapped)
        imag = jnp.where(front, swapped, value)
        tops, bottoms = [], []
        for pair in range(2):
            cosine, sine = turn_ref[2 * pair], turn_ref[2 * pair + 1]
            tops.append(cosine * real - sine * imag)
            bottoms.append(sine * real + cosine * imag)
        coeffs = jnp.concatenate(
            [jnp.concatenate(tops, axis=1), jnp.concatenate(bottoms, axis=1)], axis=0
        ).T.astype(BF16)

        total = jnp.zeros((2 * waves, 2 * BLK), F32)
        done = 0
        while done < blocks:
            take = min(4, blocks - done)
            here = slice((start + done) * BLK, (start + done + take) * BLK)
            table = table_ref[:, here]
            grid = jnp.dot(coeffs, table, preferred_element_type=F32).astype(BF16)
            mixed = jnp.dot(mix, grid, preferred_element_type=F32)
            column = (grid.astype(F32) + jnp.tanh(mixed)).astype(BF16)
            total = total + lax.dot_general(table, column, NT, preferred_element_type=F32)
            done += take
        start += blocks

        real_sum = jnp.zeros((waves, BLK), F32)
        imag_sum = jnp.zeros((waves, BLK), F32)
        for pair in range(2):
            cosine, sine = turn_ref[2 * pair], turn_ref[2 * pair + 1]
            lanes = slice(pair * BLK, (pair + 1) * BLK)
            with_cos, with_sin = total[0:waves, lanes], total[waves : 2 * waves, lanes]
            real_sum = real_sum + cosine * with_cos + sine * with_sin
            imag_sum = imag_sum + cosine * with_sin - sine * with_cos
        real_sum = real_sum + pltpu.roll(real_sum, BLK // 2, axis=1)
        imag_sum = imag_sum + pltpu.roll(imag_sum, BLK // 2, axis=1)
        result = jnp.where(front, real_sum, imag_sum) * weight_ref[fifth : fifth + 1, :]
        gathered[pl.ds(fifth, waves, stride=8), :] = result
    out_ref[...] = gathered[...].astype(BF16).reshape(out_ref.shape)


def direct_kernel(mine, place_ref, rows_ref, live_ref, out_ref):
    lev = place_ref[1]
    owner = lev if mine else lev + 1 - 2 * lax.rem(lev, 2)
    slots, cols, _ = live_ref.shape
    fields = out_ref.shape[2]
    chips, rows, _ = rows_ref.shape
    fifths = rows // (16 * slots)
    degree = lax.broadcasted_iota(jnp.int32, (cols, BLK), 0) + owner * cols
    parity = (1 - 2 * lax.rem(degree, 2)).astype(F32)
    for slot in range(slots):
        total = jnp.zeros((cols, BLK), F32)
        for fifth in range(fifths):
            start = (slot * fifths + fifth) * 16
            right = rows_ref[:, start : start + 16, :].reshape(chips * 16, BLK)
            left = live_ref[slot, :, fifth * 2 * BLK : (fifth + 1) * 2 * BLK]
            total = total + jnp.dot(left, right, preferred_element_type=F32)
        total = total + parity * pltpu.roll(total, BLK - fields, axis=1)
        turned = total.T
        for part in range(2):
            out_ref[slot, part] = turned[2 * part * fields : (2 * part + 1) * fields, :]


def local(spec_in, legendre, pattern, deal_list, circle_lengths, mixing):
    lats, levs = lax.axis_size("lat"), lax.axis_size("lev")
    chips = levs // 2
    slots, cols, half_lat = legendre.shape
    fields = spec_in.shape[2]
    waves = deal_list.shape[0]
    fifths = half_lat // (lats * levs)
    sizes = [
        -(-(5 + (half_lat // fifths) * (fifth + 1) - 1) // BLK) for fifth in range(fifths)
    ]
    place = jnp.stack([lax.axis_index("lat"), lax.axis_index("lev")]).astype(jnp.int32)
    pairs = [(lev, lev ^ 1) for lev in range(levs)]
    same_core = [[2 * chip + core for chip in range(chips)] for core in range(2)]
    rows = slots * fifths * 16

    packed = pl.pallas_call(
        pack_kernel,
        out_shape=jax.ShapeDtypeStruct((slots * (2 * fifths * cols + 2 * fields), BLK), BF16),
        in_specs=[SMEM, ANY, ANY],
        out_specs=VMEM,
        scratch_shapes=[
            pltpu.VMEM(spec_in.shape, BF16),
            pltpu.SemaphoreType.DMA((1 + slots * 2 * fifths,)),
        ],
        compiler_params=params(16),
        name="pack",
    )(place, spec_in, legendre)
    packed = lax.ppermute(packed, "lev", pairs)

    table, turns, weights, mix, own = pl.pallas_call(
        lambda *refs: table_kernel(sizes, lats, chips, half_lat, *refs),
        out_shape=(
            jax.ShapeDtypeStruct((2 * waves, sum(sizes) * BLK), BF16),
            jax.ShapeDtypeStruct((4, waves, BLK), F32),
            jax.ShapeDtypeStruct((8, BLK), F32),
            jax.ShapeDtypeStruct((8 * fields, 8 * fields), BF16),
            jax.ShapeDtypeStruct((slots, cols, fifths * 2 * BLK), BF16),
        ),
        in_specs=[SMEM, SMEM, SMEM, VMEM, ANY],
        out_specs=(VMEM,) * 5,
        scratch_shapes=[pltpu.SemaphoreType.DMA((slots * fifths,))],
        compiler_params=params(16),
        cost_estimate=pl.CostEstimate(flops=20_000_000, bytes_accessed=4_000_000, transcendentals=0),
        name="tables",
    )(place, deal_list, circle_lengths, mixing, legendre)

    partial_sums, other = pl.pallas_call(
        inverse_kernel,
        out_shape=(
            jax.ShapeDtypeStruct((chips, rows, BLK), BF16),
            jax.ShapeDtypeStruct((slots, cols, fifths * 2 * BLK), BF16),
        ),
        in_specs=[SMEM, SMEM, VMEM, VMEM, VMEM],
        out_specs=(VMEM, VMEM),
        compiler_params=params(16),
        name="inverse",
    )(place, deal_list, spec_in, own, packed)
    parts = lax.all_to_all(
        partial_sums, "lev", 0, 0, tiled=True, axis_index_groups=same_core
    )
    fourier = pl.pallas_call(
        sum_kernel,
        out_shape=jax.ShapeDtypeStruct((lats, 16, BLK), BF16),
        in_specs=[VMEM],
        out_specs=VMEM,
        scratch_shapes=[pltpu.VMEM((lats * 16, BLK), F32)],
        compiler_params=params(16),
        name="sums",
    )(parts)
    fourier = lax.all_to_all(fourier, "lat", 0, 0, tiled=True)
    analysed = pl.pallas_call(
        lambda *refs: grid_kernel(sizes, (2.0 * waves) ** (-0.5), *refs),
        out_shape=jax.ShapeDtypeStruct((lats, 16, BLK), BF16),
        in_specs=[VMEM] * 5,
        out_specs=VMEM,
        scratch_shapes=[pltpu.VMEM((lats * 16, BLK), F32), pltpu.VMEM((lats * 16, BLK), F32)],
        compiler_params=params(24),
        name="grid_rows",
    )(fourier, table, turns, weights, mix)
    analysed = lax.all_to_all(analysed, "lat", 0, 0, tiled=True)
    copies = pl.pallas_call(
        copies_kernel,
        out_shape=jax.ShapeDtypeStruct((chips, rows, BLK), BF16),
        in_specs=[VMEM],
        out_specs=VMEM,
        scratch_shapes=[pltpu.VMEM((lats * 16, BLK), F32)],
        compiler_params=params(16),
        name="copies",
    )(analysed)
    gathered = lax.all_to_all(copies, "lev", 0, 0, tiled=True, axis_index_groups=same_core)

    def direct(mine, live):
        return pl.pallas_call(
            lambda *refs: direct_kernel(mine, *refs),
            out_shape=jax.ShapeDtypeStruct((slots, 2, fields, cols), F32),
            in_specs=[SMEM, VMEM, VMEM],
            out_specs=VMEM,
            compiler_params=params(16),
            cost_estimate=pl.CostEstimate(
                flops=100_000_000, bytes_accessed=2_000_000, transcendentals=0
            ),
            name="direct_own" if mine else "direct_other",
        )(place, gathered, live)

    share = lax.ppermute(direct(False, other), "lev", pairs)
    return direct(True, own) + share


def solution(mesh):
    return jax.shard_map(
        local,
        mesh=mesh,
        in_specs=(
            P("lat", None, None, "lev"),
            P("lat", "lev", None),
            P("lat", None, None),
            P(),
            P(),
            P(),
        ),
        out_specs=P("lat", None, None, "lev"),
        check_vma=False,
    )
```

```python
import math

import jax
import jax.numpy as jnp
from jax import lax
from jax.experimental import pallas as pl
from jax.experimental.pallas import tpu as pltpu
from jax.sharding import PartitionSpec as P

BLK = 128
DEGREES = 2560
CHIPS = 16
F32 = jnp.float32
BF16 = jnp.bfloat16
VMEM = pl.BlockSpec(memory_space=pltpu.VMEM)
ANY = pl.BlockSpec(memory_space=pl.ANY)
SMEM = pl.BlockSpec(memory_space=pltpu.SMEM)
NT = (((1,), (1,)), ((), ()))


def params(kib=16384):
    return pltpu.CompilerParams(vmem_limit_bytes=kib * 1024)


def live_degrees(wave, first_col, shape):
    degree = lax.broadcasted_iota(jnp.int32, shape, 0) + first_col
    return degree // BLK * BLK <= DEGREES - 1 - wave


def mask_rows(value, wave, degrees_live, row_block, row_blocks):
    rows_live = row_block >= wave * row_blocks // (2 * DEGREES)
    flags = jnp.logical_and(degrees_live, rows_live)
    return jnp.where(flags, value, jnp.zeros_like(value))


def inverse_kernel(place_ref, deal_ref, spec_ref, own_ref, packed_ref, out_ref, other_ref):
    lat, lev = place_ref[0], place_ref[1]
    core = lax.rem(lev, 2)
    slots, _, fields, cols = spec_ref.shape
    chips = out_ref.shape[0]
    fifths = out_ref.shape[1] // (16 * slots)
    mine = lev * cols
    theirs = (lev + 1 - 2 * core) * cols

    def stacked(pieces, first_col):
        column = lax.broadcasted_iota(jnp.int32, (fields, cols), 1) + first_col
        parity = (1 - 2 * lax.rem(column, 2)).astype(F32)
        rows = []
        for piece in pieces:
            rows.append(piece)
            rows.append((piece.astype(F32) * parity).astype(BF16))
        return jnp.concatenate(rows, axis=0)

    half_rows = fifths * 2 * BLK
    for slot in range(slots):
        wave = deal_ref[slots * lat + slot]
        live = live_degrees(wave, theirs, (cols, BLK))
        left = stacked([spec_ref[slot, part] for part in range(2)], mine)
        other_left = stacked(
            [
                packed_ref[slot, part * fields : (part + 1) * fields, half_rows : half_rows + cols]
                for part in range(2)
            ],
            theirs,
        )
        for fifth in range(fifths):
            parts = []
            for half in range(2):
                begin = (2 * fifth + half) * BLK
                value = packed_ref[slot, :, begin : begin + BLK]
                row_block = 2 * fifths * core + 2 * fifth + half
                parts.append(mask_rows(value, wave, live, row_block, 4 * fifths))
            other_right = jnp.concatenate(parts, axis=1)
            here = slice(fifth * 2 * BLK, (fifth + 1) * 2 * BLK)
            other_ref[slot, :, here] = other_right
            value = jnp.dot(left, own_ref[slot, :, here], preferred_element_type=F32)
            value = value + jnp.dot(other_left, other_right, preferred_element_type=F32)
            start = (slot * fifths + fifth) * 16
            out_ref[:, start : start + 16, :] = value.T.astype(BF16).reshape(chips, 16, BLK)


def sum_kernel(in_ref, out_ref, spread):
    chips, rows, _ = in_ref.shape
    lats = out_ref.shape[0]
    groups = rows // 16
    fifths = groups // 2
    spread[...] = jnp.zeros_like(spread)
    for group in range(groups):
        piece = slice(group * 16, group * 16 + 16)
        total = in_ref[0, piece, :].astype(F32)
        for chip in range(1, chips):
            total = total + in_ref[chip, piece, :].astype(F32)
        slot, fifth = divmod(group, fifths)
        spread[pl.ds(slot * 8 + fifth, lats, stride=16), :] = total
    out_ref[...] = spread[...].astype(BF16).reshape(out_ref.shape)


def copies_kernel(in_ref, out_ref, spread):
    chips, rows, _ = out_ref.shape
    lats = in_ref.shape[0]
    groups = rows // 16
    fifths = groups // 2
    spread[...] = in_ref[...].astype(F32).reshape(spread.shape)
    for group in range(groups):
        slot, fifth = divmod(group, fifths)
        value = spread[pl.ds(slot * 8 + fifth, lats, stride=16), :].astype(BF16)
        for chip in range(chips):
            out_ref[chip, group * 16 : group * 16 + 16, :] = value


def circle(x, length):
    quarter = length * 0.25
    per = 1.0 / quarter
    turns = jnp.floor(x * per + 0.5)
    rest = x - turns * quarter
    more = jnp.floor(rest * per + 0.5)
    rest = rest - more * quarter
    turns = turns + more
    turns = turns - 4.0 * jnp.floor(turns * 0.25)
    angle = rest * ((2.0 * math.pi) / length)
    sq = angle * angle
    sine = angle * (
        1.0 + sq * (-1.0 / 6 + sq * (1.0 / 120 + sq * (-1.0 / 5040 + sq * (1.0 / 362880))))
    )
    cosine = 1.0 + sq * (
        -0.5 + sq * (1.0 / 24 + sq * (-1.0 / 720 + sq * (1.0 / 40320 + sq * (-1.0 / 3628800))))
    )
    odd = (turns == 1.0) | (turns == 3.0)
    first = jnp.where(odd, sine, cosine)
    second = jnp.where(odd, cosine, sine)
    first = jnp.where((turns == 1.0) | (turns == 2.0), -first, first)
    second = jnp.where(turns >= 2.0, -second, second)
    return first, second


def widths(core, fifths):
    return [2 * BLK * (core * fifths + fifth + 1) for fifth in range(fifths)]


def table_kernel(fifths, place_ref, deal_ref, lengths_ref, mixing_ref, leg_ref,
                 table_ref, turn_ref, weight_ref, mix_ref, gram_ref, own_ref, sems):
    lat, lev = place_ref[0], place_ref[1]
    core = lax.rem(lev, 2)
    slots, cols, half_lat = leg_ref.shape
    half_rows = half_lat // 2
    copies = []
    for slot in range(slots):
        begin = pl.multiple_of(core * half_rows, BLK)
        copies.append(
            pltpu.make_async_copy(
                leg_ref.at[slot, :, pl.ds(begin, half_rows)], own_ref.at[slot], sems.at[slot]
            )
        )
        copies[-1].start()
    waves = deal_ref.shape[0]
    fields = mixing_ref.shape[0]
    shape = (waves, BLK)
    sub = lax.broadcasted_iota(jnp.int32, shape, 0)
    lane = lax.broadcasted_iota(jnp.int32, shape, 1)
    lane_f = lane.astype(F32)
    wave = jnp.zeros(shape, jnp.int32)
    for slot in range(waves):
        wave = jnp.where(sub == slot, deal_ref[slot], wave)
    wave_f = wave.astype(F32)
    for pair in range(2):
        quarter = 2 * pair + (lane >= BLK // 2).astype(jnp.int32)
        turn = lax.rem(quarter * wave, 4)
        turn_ref[2 * pair] = jnp.where(turn == 0, 1.0, jnp.where(turn == 2, -1.0, 0.0))
        turn_ref[2 * pair + 1] = jnp.where(turn == 1, 1.0, jnp.where(turn == 3, -1.0, 0.0))
    size = mix_ref.shape[0]
    pick = (
        lax.rem(lax.broadcasted_iota(jnp.int32, (size, fields), 0), fields)
        == lax.broadcasted_iota(jnp.int32, (size, fields), 1)
    ).astype(F32).astype(BF16)
    tall = jnp.dot(pick, mixing_ref[...], preferred_element_type=F32).astype(BF16)
    wide = lax.dot_general(tall, pick, NT, preferred_element_type=F32)
    same = (
        lax.broadcasted_iota(jnp.int32, (size, size), 0) // fields
        == lax.broadcasted_iota(jnp.int32, (size, size), 1) // fields
    )
    mix_ref[...] = jnp.where(same, wide, 0.0).astype(BF16)
    weight_ref[...] = jnp.zeros_like(weight_ref)
    group = half_rows // fifths
    first_row = core * half_rows + (lev // 2) * (2 * BLK // CHIPS) + lat

    def build(which):
        main = widths(which, fifths)
        extra = sum(main)
        start = 0
        for fifth, width in enumerate(main):
            row = first_row + fifth * group
            length = lengths_ref[row]
            points = length // 4
            length_f = jnp.full(shape, length, jnp.int32).astype(F32)
            low_cos, low_sin = circle(wave_f * lane_f, length_f)
            high_cos, high_sin = circle(wave_f * lane_f * float(BLK), length_f)
            blocks = width // BLK
            for block in range(blocks + 1):
                a_cos = jnp.broadcast_to(high_cos[:, block : block + 1], shape)
                a_sin = jnp.broadcast_to(high_sin[:, block : block + 1], shape)
                cosine = a_cos * low_cos - a_sin * low_sin
                sine = a_sin * low_cos + a_cos * low_sin
                inside = lane + block * BLK < points
                begin = start + block * BLK if block < blocks else extra + fifth * BLK
                here = slice(begin, begin + BLK)
                table_ref[0:waves, here] = jnp.where(inside, cosine, 0.0).astype(BF16)
                table_ref[waves : 2 * waves, here] = jnp.where(inside, -sine, 0.0).astype(BF16)
            row_f = jnp.full((1, BLK), row, jnp.int32).astype(F32) + 0.5
            _, sine = circle(row_f, jnp.full((1, BLK), 4.0 * half_lat, F32))
            weight_ref[fifth : fifth + 1, :] = sine / jnp.sqrt(length_f[0:1, :])
            start += width
        start = 0
        for fifth, width in enumerate(main):
            table = table_ref[:, start : start + width]
            gram = lax.dot_general(table, table, NT, preferred_element_type=F32)
            table = table_ref[:, extra + fifth * BLK : extra + (fifth + 1) * BLK]
            gram = gram + lax.dot_general(table, table, NT, preferred_element_type=F32)
            gram_ref[fifth] = two_terms(gram)
            start += width

    pl.when(core == 0)(lambda: build(0))
    pl.when(core == 1)(lambda: build(1))
    for copy in copies:
        copy.wait()
    for slot in range(slots):
        number = deal_ref[slots * lat + slot]
        live = live_degrees(number, lev * cols, (cols, BLK))
        for block in range(2 * fifths):
            here = slice(block * BLK, (block + 1) * BLK)
            row_block = 2 * fifths * core + block
            own_ref[slot, :, here] = mask_rows(
                own_ref[slot, :, here], number, live, row_block, 4 * fifths
            )


def two_terms(value):
    high = value.astype(BF16)
    low = (value - high.astype(F32)).astype(BF16)
    return jnp.concatenate([high, low], axis=1)


def grid_kernel(scale, place_ref, lengths_ref, in_ref, table_ref, turn_ref, weight_ref, mix_ref, gram_ref,
                out_ref, spread, gathered, totals, mixed_coeffs):
    fifths = gram_ref.shape[0]
    waves = turn_ref.shape[1]
    core = lax.rem(place_ref[1], 2)
    lane = lax.broadcasted_iota(jnp.int32, (waves, BLK), 1)
    front = lane < BLK // 2
    spread[...] = in_ref[...].astype(F32).reshape(spread.shape)
    gathered[...] = jnp.zeros_like(gathered)
    mix = mix_ref[...]
    group = 2 * BLK
    first_row = core * fifths * group + (place_ref[1] // 2) * (group // CHIPS) + place_ref[0]

    def analysed(table, fifth):
        twice = jnp.concatenate([table, table], axis=0)
        mixed = jnp.dot(mixed_coeffs[fifth], twice, preferred_element_type=F32)
        change = jnp.tanh(mixed).astype(BF16)
        return lax.dot_general(table, change, NT, preferred_element_type=F32)

    for fifth in range(fifths):
        value = spread[pl.ds(fifth, waves, stride=8), :] * scale
        swapped = pltpu.roll(value, BLK // 2, axis=1)
        real = jnp.where(front, value, swapped)
        imag = jnp.where(front, swapped, value)
        tops, bottoms = [], []
        for pair in range(2):
            cosine, sine = turn_ref[2 * pair], turn_ref[2 * pair + 1]
            tops.append(cosine * real - sine * imag)
            bottoms.append(sine * real + cosine * imag)
        coeffs = jnp.concatenate(
            [jnp.concatenate(tops, axis=1), jnp.concatenate(bottoms, axis=1)], axis=0
        ).astype(BF16)
        mixed_coeffs[fifth] = two_terms(
            lax.dot_general(mix, coeffs, NT, preferred_element_type=F32)
        )
        totals[fifth] = jnp.dot(
            gram_ref[fifth], jnp.concatenate([coeffs, coeffs], axis=0), preferred_element_type=F32
        )

    def rows(which):
        main = widths(which, fifths)
        start = 0
        for fifth, width in enumerate(main):
            total = totals[fifth]
            for begin in range(start, start + width, 4 * BLK):
                end = min(begin + 4 * BLK, start + width)
                total = total + analysed(table_ref[:, begin:end], fifth)
            totals[fifth] = total
            start += width
        for fifth, width in enumerate(main):
            begin = start + fifth * BLK
            points = lengths_ref[first_row + fifth * group] // 4

            @pl.when(points > width)
            def _():
                totals[fifth] += analysed(table_ref[:, begin : begin + BLK], fifth)

    pl.when(core == 0)(lambda: rows(0))
    pl.when(core == 1)(lambda: rows(1))

    for fifth in range(fifths):
        total = totals[fifth]
        real_sum = jnp.zeros((waves, BLK), F32)
        imag_sum = jnp.zeros((waves, BLK), F32)
        for pair in range(2):
            cosine, sine = turn_ref[2 * pair], turn_ref[2 * pair + 1]
            lanes = slice(pair * BLK, (pair + 1) * BLK)
            with_cos, with_sin = total[0:waves, lanes], total[waves : 2 * waves, lanes]
            real_sum = real_sum + cosine * with_cos + sine * with_sin
            imag_sum = imag_sum + cosine * with_sin - sine * with_cos
        real_sum = real_sum + pltpu.roll(real_sum, BLK // 2, axis=1)
        imag_sum = imag_sum + pltpu.roll(imag_sum, BLK // 2, axis=1)
        result = jnp.where(front, real_sum, imag_sum) * weight_ref[fifth : fifth + 1, :]
        gathered[pl.ds(fifth, waves, stride=8), :] = result
    out_ref[...] = gathered[...].astype(BF16).reshape(out_ref.shape)


def direct_kernel(mine, place_ref, rows_ref, live_ref, out_ref):
    lev = place_ref[1]
    owner = lev if mine else lev + 1 - 2 * lax.rem(lev, 2)
    slots, cols, _ = live_ref.shape
    fields = out_ref.shape[2]
    chips, rows, _ = rows_ref.shape
    fifths = rows // (16 * slots)
    degree = lax.broadcasted_iota(jnp.int32, (cols, BLK), 0) + owner * cols
    parity = (1 - 2 * lax.rem(degree, 2)).astype(F32)
    for slot in range(slots):
        total = jnp.zeros((cols, BLK), F32)
        for fifth in range(fifths):
            start = (slot * fifths + fifth) * 16
            right = rows_ref[:, start : start + 16, :].reshape(chips * 16, BLK)
            left = live_ref[slot, :, fifth * 2 * BLK : (fifth + 1) * 2 * BLK]
            total = total + jnp.dot(left, right, preferred_element_type=F32)
        total = total + parity * pltpu.roll(total, BLK - fields, axis=1)
        turned = total.T
        for part in range(2):
            out_ref[slot, part] = turned[2 * part * fields : (2 * part + 1) * fields, :]


def local(spec_in, legendre, pattern, deal_list, circle_lengths, mixing):
    lats, levs = lax.axis_size("lat"), lax.axis_size("lev")
    chips = levs // 2
    slots, cols, half_lat = legendre.shape
    fields = spec_in.shape[2]
    waves = deal_list.shape[0]
    fifths = half_lat // (lats * levs)
    place = jnp.stack([lax.axis_index("lat"), lax.axis_index("lev")]).astype(jnp.int32)
    pairs = [(lev, lev ^ 1) for lev in range(levs)]
    same_core = [[2 * chip + core for chip in range(chips)] for core in range(2)]
    rows = slots * fifths * 16

    half = half_lat // 2
    packed = jnp.concatenate(
        [
            jnp.where(lax.axis_index("lev") & 1 == 0, legendre[:, :, half:], legendre[:, :, :half]),
            jnp.pad(
                spec_in.reshape(slots, 2 * fields, cols),
                ((0, 0), (0, cols - 2 * fields), (0, BLK - cols)),
            ),
        ],
        axis=2,
    )
    packed = lax.ppermute(packed, "lev", pairs)

    table, turns, weights, mix, grams, own = pl.pallas_call(
        lambda *refs: table_kernel(fifths, *refs),
        out_shape=(
            jax.ShapeDtypeStruct((2 * waves, sum(widths(1, fifths)) + fifths * BLK), BF16),
            jax.ShapeDtypeStruct((4, waves, BLK), F32),
            jax.ShapeDtypeStruct((8, BLK), F32),
            jax.ShapeDtypeStruct((8 * fields, 8 * fields), BF16),
            jax.ShapeDtypeStruct((fifths, 2 * waves, BLK), BF16),
            jax.ShapeDtypeStruct((slots, cols, fifths * 2 * BLK), BF16),
        ),
        in_specs=[SMEM, SMEM, SMEM, VMEM, ANY],
        out_specs=(VMEM,) * 6,
        scratch_shapes=[pltpu.SemaphoreType.DMA((slots,))],
        compiler_params=params(),
        cost_estimate=pl.CostEstimate(flops=20_000_000, bytes_accessed=4_000_000, transcendentals=0),
        name="tables",
    )(place, deal_list, circle_lengths, mixing, legendre)

    partial_sums, other = pl.pallas_call(
        inverse_kernel,
        out_shape=(
            jax.ShapeDtypeStruct((chips, rows, BLK), BF16),
            jax.ShapeDtypeStruct((slots, cols, fifths * 2 * BLK), BF16),
        ),
        in_specs=[SMEM, SMEM, VMEM, VMEM, VMEM],
        out_specs=(VMEM, VMEM),
        compiler_params=params(),
        name="inverse",
    )(place, deal_list, spec_in, own, packed)
    parts = lax.all_to_all(
        partial_sums, "lev", 0, 0, tiled=True, axis_index_groups=same_core
    )
    fourier = pl.pallas_call(
        sum_kernel,
        out_shape=jax.ShapeDtypeStruct((lats, 16, BLK), BF16),
        in_specs=[VMEM],
        out_specs=VMEM,
        scratch_shapes=[pltpu.VMEM((lats * 16, BLK), F32)],
        compiler_params=params(),
        name="sums",
    )(parts)
    fourier = lax.all_to_all(fourier, "lat", 0, 0, tiled=True)
    analysed = pl.pallas_call(
        lambda *refs: grid_kernel((2.0 * waves) ** (-0.5), *refs),
        out_shape=jax.ShapeDtypeStruct((lats, 16, BLK), BF16),
        in_specs=[SMEM, SMEM] + [VMEM] * 6,
        out_specs=VMEM,
        scratch_shapes=[
            pltpu.VMEM((lats * 16, BLK), F32),
            pltpu.VMEM((lats * 16, BLK), F32),
            pltpu.VMEM((fifths, 2 * waves, 8 * fields), F32),
            pltpu.VMEM((fifths, 8 * fields, BLK), BF16),
        ],
        compiler_params=params(24576),
        name="grid_rows",
    )(place, circle_lengths, fourier, table, turns, weights, mix, grams)
    analysed = lax.all_to_all(analysed, "lat", 0, 0, tiled=True)
    copies = pl.pallas_call(
        copies_kernel,
        out_shape=jax.ShapeDtypeStruct((chips, rows, BLK), BF16),
        in_specs=[VMEM],
        out_specs=VMEM,
        scratch_shapes=[pltpu.VMEM((lats * 16, BLK), F32)],
        compiler_params=params(),
        name="copies",
    )(analysed)
    gathered = lax.all_to_all(copies, "lev", 0, 0, tiled=True, axis_index_groups=same_core)

    def direct(mine, live):
        return pl.pallas_call(
            lambda *refs: direct_kernel(mine, *refs),
            out_shape=jax.ShapeDtypeStruct((slots, 2, fields, cols), F32),
            in_specs=[SMEM, VMEM, VMEM],
            out_specs=VMEM,
            compiler_params=params(),
            cost_estimate=pl.CostEstimate(
                flops=100_000_000, bytes_accessed=2_000_000, transcendentals=0
            ),
            name="direct_own" if mine else "direct_other",
        )(place, gathered, live)

    share = lax.ppermute(direct(False, other), "lev", pairs)
    return direct(True, own) + share


def solution(mesh):
    return jax.shard_map(
        local,
        mesh=mesh,
        in_specs=(
            P("lat", None, None, "lev"),
            P("lat", "lev", None),
            P("lat", None, None),
            P(),
            P(),
            P(),
        ),
        out_specs=P("lat", None, None, "lev"),
        check_vma=False,
    )
```

```python
import math

import jax
import jax.numpy as jnp
from jax import lax
from jax.experimental import pallas as pl
from jax.experimental.pallas import tpu as pltpu
from jax.sharding import PartitionSpec as P

BLK = 128
DEGREES = 2560
CHIPS = 16
F32 = jnp.float32
BF16 = jnp.bfloat16
VMEM = pl.BlockSpec(memory_space=pltpu.VMEM)
SMEM = pl.BlockSpec(memory_space=pltpu.SMEM)
NT = (((1,), (1,)), ((), ()))


def params(kib=16384):
    return pltpu.CompilerParams(vmem_limit_bytes=kib * 1024)


def wave_of(deal_ref, slot):
    deal = deal_ref[...]
    here = lax.broadcasted_iota(jnp.int32, deal.shape, 1) == slot
    return jnp.sum(jnp.where(here, deal, 0).astype(F32), axis=1, keepdims=True).astype(jnp.int32)


def live_degrees(wave, first_col, shape):
    degree = lax.broadcasted_iota(jnp.int32, shape, 0) + first_col
    return degree // BLK * BLK <= DEGREES - 1 - wave


def mask_rows(value, wave, degrees_live, row_block, row_blocks):
    rows_live = row_block >= wave * row_blocks // (2 * DEGREES)
    flags = jnp.logical_and(degrees_live, rows_live)
    return jnp.where(flags, value, jnp.zeros_like(value))


def inverse_kernel(deal_ref, spec_ref, own_ref, packed_ref, out_ref, other_ref):
    lat, lev = lax.axis_index("lat"), lax.axis_index("lev")
    core = lax.rem(lev, 2)
    slots, _, fields, cols = spec_ref.shape
    chips = out_ref.shape[0]
    fifths = out_ref.shape[1] // (16 * slots)
    mine = lev * cols
    theirs = (lev + 1 - 2 * core) * cols

    def stacked(pieces, first_col):
        column = lax.broadcasted_iota(jnp.int32, (fields, cols), 1) + first_col
        parity = (1 - 2 * lax.rem(column, 2)).astype(F32)
        rows = []
        for piece in pieces:
            rows.append(piece)
            rows.append((piece.astype(F32) * parity).astype(BF16))
        return jnp.concatenate(rows, axis=0)

    half_rows = fifths * 2 * BLK
    for slot in range(slots):
        wave = wave_of(deal_ref, slots * lat + slot)
        live = live_degrees(wave, theirs, (cols, BLK))
        left = stacked([spec_ref[slot, part] for part in range(2)], mine)
        other_left = stacked(
            [
                packed_ref[slot, part * fields : (part + 1) * fields, half_rows : half_rows + cols]
                for part in range(2)
            ],
            theirs,
        )
        for fifth in range(fifths):
            parts = []
            for half in range(2):
                begin = (2 * fifth + half) * BLK
                value = packed_ref[slot, :, begin : begin + BLK]
                row_block = 2 * fifths * core + 2 * fifth + half
                parts.append(mask_rows(value, wave, live, row_block, 4 * fifths))
            other_right = jnp.concatenate(parts, axis=1)
            here = slice(fifth * 2 * BLK, (fifth + 1) * 2 * BLK)
            other_ref[slot, :, here] = other_right
            value = jnp.dot(left, own_ref[slot, :, here], preferred_element_type=F32)
            value = value + jnp.dot(other_left, other_right, preferred_element_type=F32)
            start = (slot * fifths + fifth) * 16
            out_ref[:, start : start + 16, :] = value.T.astype(BF16).reshape(chips, 16, BLK)


def sum_kernel(in_ref, out_ref, spread):
    chips, rows, _ = in_ref.shape
    lats = out_ref.shape[0]
    groups = rows // 16
    fifths = groups // 2
    spread[...] = jnp.zeros_like(spread)
    for group in range(groups):
        piece = slice(group * 16, group * 16 + 16)
        total = in_ref[0, piece, :].astype(F32)
        for chip in range(1, chips):
            total = total + in_ref[chip, piece, :].astype(F32)
        slot, fifth = divmod(group, fifths)
        spread[pl.ds(slot * 8 + fifth, lats, stride=16), :] = total
    out_ref[...] = spread[...].astype(BF16).reshape(out_ref.shape)


def copies_kernel(in_ref, out_ref, spread):
    chips, rows, _ = out_ref.shape
    lats = in_ref.shape[0]
    groups = rows // 16
    fifths = groups // 2
    spread[...] = in_ref[...].astype(F32).reshape(spread.shape)
    for group in range(groups):
        slot, fifth = divmod(group, fifths)
        value = spread[pl.ds(slot * 8 + fifth, lats, stride=16), :].astype(BF16)
        for chip in range(chips):
            out_ref[chip, group * 16 : group * 16 + 16, :] = value


def circle(x, length):
    quarter = length * 0.25
    per = 1.0 / quarter
    turns = jnp.floor(x * per + 0.5)
    rest = x - turns * quarter
    more = jnp.floor(rest * per + 0.5)
    rest = rest - more * quarter
    turns = turns + more
    turns = turns - 4.0 * jnp.floor(turns * 0.25)
    angle = rest * ((2.0 * math.pi) / length)
    sq = angle * angle
    sine = angle * (
        1.0 + sq * (-1.0 / 6 + sq * (1.0 / 120 + sq * (-1.0 / 5040 + sq * (1.0 / 362880))))
    )
    cosine = 1.0 + sq * (
        -0.5 + sq * (1.0 / 24 + sq * (-1.0 / 720 + sq * (1.0 / 40320 + sq * (-1.0 / 3628800))))
    )
    odd = (turns == 1.0) | (turns == 3.0)
    first = jnp.where(odd, sine, cosine)
    second = jnp.where(odd, cosine, sine)
    first = jnp.where((turns == 1.0) | (turns == 2.0), -first, first)
    second = jnp.where(turns >= 2.0, -second, second)
    return first, second


def widths(core, fifths):
    return [2 * BLK * (core * fifths + fifth + 1) for fifth in range(fifths)]


def own_kernel(deal_ref, leg_ref, own_ref):
    lat, lev = lax.axis_index("lat"), lax.axis_index("lev")
    core = lax.rem(lev, 2)
    slots, cols, half_rows = own_ref.shape
    blocks = half_rows // BLK
    for slot in range(slots):
        wave = wave_of(deal_ref, slots * lat + slot)
        live = live_degrees(wave, lev * cols, (cols, BLK))
        for block in range(blocks):
            row_block = blocks * core + block
            value = leg_ref[slot, :, pl.ds(pl.multiple_of(row_block * BLK, BLK), BLK)]
            own_ref[slot, :, block * BLK : (block + 1) * BLK] = mask_rows(
                value, wave, live, row_block, 2 * blocks
            )


def table_kernel(fifths, deal_ref, lengths_ref, mixing_ref,
                 table_ref, turn_ref, weight_ref, mix_ref, gram_ref):
    lat, lev = lax.axis_index("lat"), lax.axis_index("lev")
    core = lax.rem(lev, 2)
    half_lat = lengths_ref.shape[0]
    half_rows = half_lat // 2
    waves = deal_ref.shape[0]
    fields = mixing_ref.shape[0]
    shape = (waves, BLK)
    sub = lax.broadcasted_iota(jnp.int32, shape, 0)
    lane = lax.broadcasted_iota(jnp.int32, shape, 1)
    lane_f = lane.astype(F32)
    wave = jnp.zeros(shape, jnp.int32)
    for slot in range(waves):
        wave = jnp.where(sub == slot, deal_ref[slot], wave)
    wave_f = wave.astype(F32)
    for pair in range(2):
        quarter = 2 * pair + (lane >= BLK // 2).astype(jnp.int32)
        turn = lax.rem(quarter * wave, 4)
        turn_ref[2 * pair] = jnp.where(turn == 0, 1.0, jnp.where(turn == 2, -1.0, 0.0))
        turn_ref[2 * pair + 1] = jnp.where(turn == 1, 1.0, jnp.where(turn == 3, -1.0, 0.0))
    size = mix_ref.shape[0]
    pick = (
        lax.rem(lax.broadcasted_iota(jnp.int32, (size, fields), 0), fields)
        == lax.broadcasted_iota(jnp.int32, (size, fields), 1)
    ).astype(F32).astype(BF16)
    tall = jnp.dot(pick, mixing_ref[...], preferred_element_type=F32).astype(BF16)
    wide = lax.dot_general(tall, pick, NT, preferred_element_type=F32)
    same = (
        lax.broadcasted_iota(jnp.int32, (size, size), 0) // fields
        == lax.broadcasted_iota(jnp.int32, (size, size), 1) // fields
    )
    mix_ref[...] = jnp.where(same, wide, 0.0).astype(BF16)
    weight_ref[...] = jnp.zeros_like(weight_ref)
    group = half_rows // fifths
    first_row = core * half_rows + (lev // 2) * (2 * BLK // CHIPS) + lat

    def build(which):
        main = widths(which, fifths)
        extra = sum(main)
        start = 0
        beyond = 0
        for fifth, width in enumerate(main):
            row = first_row + fifth * group
            length = lengths_ref[row]
            points = length // 4
            beyond = jnp.maximum(beyond, points - width)
            length_f = jnp.full(shape, length, jnp.int32).astype(F32)
            low_cos, low_sin = circle(wave_f * lane_f, length_f)
            high_cos, high_sin = circle(wave_f * lane_f * float(BLK), length_f)
            blocks = width // BLK
            for block in range(blocks + 1):
                a_cos = jnp.broadcast_to(high_cos[:, block : block + 1], shape)
                a_sin = jnp.broadcast_to(high_sin[:, block : block + 1], shape)
                cosine = a_cos * low_cos - a_sin * low_sin
                sine = a_sin * low_cos + a_cos * low_sin
                inside = lane + block * BLK < points
                begin = start + block * BLK if block < blocks else extra + fifth * BLK
                here = slice(begin, begin + BLK)
                table_ref[0:waves, here] = jnp.where(inside, cosine, 0.0).astype(BF16)
                table_ref[waves : 2 * waves, here] = jnp.where(inside, -sine, 0.0).astype(BF16)
            row_f = jnp.full((1, BLK), row, jnp.int32).astype(F32) + 0.5
            _, sine = circle(row_f, jnp.full((1, BLK), 4.0 * half_lat, F32))
            weight_ref[fifth : fifth + 1, :] = sine / jnp.sqrt(length_f[0:1, :])
            start += width
        weight_ref[fifths : fifths + 1, :] = jnp.full((1, BLK), beyond, jnp.int32).astype(F32)
        start = 0
        for fifth, width in enumerate(main):
            table = table_ref[:, start : start + width]
            gram = lax.dot_general(table, table, NT, preferred_element_type=F32)
            table = table_ref[:, extra + fifth * BLK : extra + (fifth + 1) * BLK]
            gram = gram + lax.dot_general(table, table, NT, preferred_element_type=F32)
            gram_ref[fifth] = two_terms(gram)
            start += width

    pl.when(core == 0)(lambda: build(0))
    pl.when(core == 1)(lambda: build(1))


def two_terms(value):
    high = value.astype(BF16)
    low = (value - high.astype(F32)).astype(BF16)
    return jnp.concatenate([high, low], axis=1)


def grid_kernel(scale, in_ref, table_ref, turn_ref, weight_ref, mix_ref, gram_ref,
                out_ref, spread, gathered, totals, mixed_coeffs):
    fifths = gram_ref.shape[0]
    waves = turn_ref.shape[1]
    core = lax.rem(lax.axis_index("lev"), 2)
    beyond = jnp.max(weight_ref[fifths : fifths + 1, :])
    lane = lax.broadcasted_iota(jnp.int32, (waves, BLK), 1)
    front = lane < BLK // 2
    spread[...] = in_ref[...].astype(F32).reshape(spread.shape)
    gathered[...] = jnp.zeros_like(gathered)
    mix = mix_ref[...]

    def analysed(table, fifth):
        twice = jnp.concatenate([table, table], axis=0)
        mixed = jnp.dot(mixed_coeffs[fifth], twice, preferred_element_type=F32)
        change = jnp.tanh(mixed).astype(BF16)
        return lax.dot_general(table, change, NT, preferred_element_type=F32)

    for fifth in range(fifths):
        value = spread[pl.ds(fifth, waves, stride=8), :] * scale
        swapped = pltpu.roll(value, BLK // 2, axis=1)
        real = jnp.where(front, value, swapped)
        imag = jnp.where(front, swapped, value)
        tops, bottoms = [], []
        for pair in range(2):
            cosine, sine = turn_ref[2 * pair], turn_ref[2 * pair + 1]
            tops.append(cosine * real - sine * imag)
            bottoms.append(sine * real + cosine * imag)
        coeffs = jnp.concatenate(
            [jnp.concatenate(tops, axis=1), jnp.concatenate(bottoms, axis=1)], axis=0
        ).astype(BF16)
        mixed_coeffs[fifth] = two_terms(
            lax.dot_general(mix, coeffs, NT, preferred_element_type=F32)
        )
        totals[fifth] = jnp.dot(
            gram_ref[fifth], jnp.concatenate([coeffs, coeffs], axis=0), preferred_element_type=F32
        )

    def rows(which):
        main = widths(which, fifths)
        start = 0
        for fifth, width in enumerate(main):
            total = totals[fifth]
            for begin in range(start, start + width, 4 * BLK):
                end = min(begin + 4 * BLK, start + width)
                total = total + analysed(table_ref[:, begin:end], fifth)
            totals[fifth] = total
            start += width
        @pl.when(beyond > 0.0)
        def _():
            for fifth in range(fifths):
                begin = start + fifth * BLK
                totals[fifth] += analysed(table_ref[:, begin : begin + BLK], fifth)

    pl.when(core == 0)(lambda: rows(0))
    pl.when(core == 1)(lambda: rows(1))

    for fifth in range(fifths):
        total = totals[fifth]
        real_sum = jnp.zeros((waves, BLK), F32)
        imag_sum = jnp.zeros((waves, BLK), F32)
        for pair in range(2):
            cosine, sine = turn_ref[2 * pair], turn_ref[2 * pair + 1]
            lanes = slice(pair * BLK, (pair + 1) * BLK)
            with_cos, with_sin = total[0:waves, lanes], total[waves : 2 * waves, lanes]
            real_sum = real_sum + cosine * with_cos + sine * with_sin
            imag_sum = imag_sum + cosine * with_sin - sine * with_cos
        real_sum = real_sum + pltpu.roll(real_sum, BLK // 2, axis=1)
        imag_sum = imag_sum + pltpu.roll(imag_sum, BLK // 2, axis=1)
        result = jnp.where(front, real_sum, imag_sum) * weight_ref[fifth : fifth + 1, :]
        gathered[pl.ds(fifth, waves, stride=8), :] = result
    out_ref[...] = gathered[...].astype(BF16).reshape(out_ref.shape)


def direct_kernel(mine, rows_ref, live_ref, out_ref):
    lev = lax.axis_index("lev")
    owner = lev if mine else lev + 1 - 2 * lax.rem(lev, 2)
    slots, cols, _ = live_ref.shape
    fields = out_ref.shape[2]
    chips, rows, _ = rows_ref.shape
    fifths = rows // (16 * slots)
    degree = lax.broadcasted_iota(jnp.int32, (cols, BLK), 0) + owner * cols
    parity = (1 - 2 * lax.rem(degree, 2)).astype(F32)
    for slot in range(slots):
        total = jnp.zeros((cols, BLK), F32)
        for fifth in range(fifths):
            start = (slot * fifths + fifth) * 16
            right = rows_ref[:, start : start + 16, :].reshape(chips * 16, BLK)
            left = live_ref[slot, :, fifth * 2 * BLK : (fifth + 1) * 2 * BLK]
            total = total + jnp.dot(left, right, preferred_element_type=F32)
        total = total + parity * pltpu.roll(total, BLK - fields, axis=1)
        turned = total.T
        for part in range(2):
            out_ref[slot, part] = turned[2 * part * fields : (2 * part + 1) * fields, :]


def local(spec_in, legendre, pattern, deal_list, circle_lengths, mixing):
    lats, levs = lax.axis_size("lat"), lax.axis_size("lev")
    chips = levs // 2
    slots, cols, half_lat = legendre.shape
    fields = spec_in.shape[2]
    waves = deal_list.shape[0]
    fifths = half_lat // (lats * levs)
    pairs = [(lev, lev ^ 1) for lev in range(levs)]
    same_core = [[2 * chip + core for chip in range(chips)] for core in range(2)]
    rows = slots * fifths * 16

    deal_row = deal_list.reshape(1, waves)
    half = half_lat // 2
    packed = jnp.concatenate(
        [
            jnp.where(lax.axis_index("lev") & 1 == 0, legendre[:, :, half:], legendre[:, :, :half]),
            jnp.pad(
                spec_in.reshape(slots, 2 * fields, cols),
                ((0, 0), (0, cols - 2 * fields), (0, BLK - cols)),
            ),
        ],
        axis=2,
    )
    packed = lax.ppermute(packed, "lev", pairs)

    table, turns, weights, mix, grams = pl.pallas_call(
        lambda *refs: table_kernel(fifths, *refs),
        out_shape=(
            jax.ShapeDtypeStruct((2 * waves, sum(widths(1, fifths)) + fifths * BLK), BF16),
            jax.ShapeDtypeStruct((4, waves, BLK), F32),
            jax.ShapeDtypeStruct((8, BLK), F32),
            jax.ShapeDtypeStruct((8 * fields, 8 * fields), BF16),
            jax.ShapeDtypeStruct((fifths, 2 * waves, BLK), BF16),
        ),
        in_specs=[SMEM, SMEM, VMEM],
        out_specs=(VMEM,) * 5,
        compiler_params=params(),
        cost_estimate=pl.CostEstimate(flops=20_000_000, bytes_accessed=4_000_000, transcendentals=0),
        name="tables",
    )(deal_list, circle_lengths, mixing)
    own = pl.pallas_call(
        own_kernel,
        out_shape=jax.ShapeDtypeStruct((slots, cols, fifths * 2 * BLK), BF16),
        in_specs=[VMEM, VMEM],
        out_specs=VMEM,
        compiler_params=params(),
        cost_estimate=pl.CostEstimate(flops=1_000_000, bytes_accessed=1_300_000, transcendentals=0),
        name="own",
    )(deal_row, legendre)

    partial_sums, other = pl.pallas_call(
        inverse_kernel,
        out_shape=(
            jax.ShapeDtypeStruct((chips, rows, BLK), BF16),
            jax.ShapeDtypeStruct((slots, cols, fifths * 2 * BLK), BF16),
        ),
        in_specs=[VMEM] * 4,
        out_specs=(VMEM, VMEM),
        compiler_params=params(),
        name="inverse",
    )(deal_row, spec_in, own, packed)
    parts = lax.all_to_all(
        partial_sums, "lev", 0, 0, tiled=True, axis_index_groups=same_core
    )
    fourier = pl.pallas_call(
        sum_kernel,
        out_shape=jax.ShapeDtypeStruct((lats, 16, BLK), BF16),
        in_specs=[VMEM],
        out_specs=VMEM,
        scratch_shapes=[pltpu.VMEM((lats * 16, BLK), F32)],
        compiler_params=params(),
        name="sums",
    )(parts)
    fourier = lax.all_to_all(fourier, "lat", 0, 0, tiled=True)
    analysed = pl.pallas_call(
        lambda *refs: grid_kernel((2.0 * waves) ** (-0.5), *refs),
        out_shape=jax.ShapeDtypeStruct((lats, 16, BLK), BF16),
        in_specs=[VMEM] * 6,
        out_specs=VMEM,
        scratch_shapes=[
            pltpu.VMEM((lats * 16, BLK), F32),
            pltpu.VMEM((lats * 16, BLK), F32),
            pltpu.VMEM((fifths, 2 * waves, 8 * fields), F32),
            pltpu.VMEM((fifths, 8 * fields, BLK), BF16),
        ],
        compiler_params=params(24576),
        name="grid_rows",
    )(fourier, table, turns, weights, mix, grams)
    analysed = lax.all_to_all(analysed, "lat", 0, 0, tiled=True)
    copies = pl.pallas_call(
        copies_kernel,
        out_shape=jax.ShapeDtypeStruct((chips, rows, BLK), BF16),
        in_specs=[VMEM],
        out_specs=VMEM,
        scratch_shapes=[pltpu.VMEM((lats * 16, BLK), F32)],
        compiler_params=params(),
        name="copies",
    )(analysed)
    gathered = lax.all_to_all(copies, "lev", 0, 0, tiled=True, axis_index_groups=same_core)

    def direct(mine, live):
        return pl.pallas_call(
            lambda *refs: direct_kernel(mine, *refs),
            out_shape=jax.ShapeDtypeStruct((slots, 2, fields, cols), F32),
            in_specs=[VMEM, VMEM],
            out_specs=VMEM,
            compiler_params=params(),
            cost_estimate=pl.CostEstimate(
                flops=100_000_000, bytes_accessed=2_000_000, transcendentals=0
            ),
            name="direct_own" if mine else "direct_other",
        )(gathered, live)

    share = lax.ppermute(direct(False, other), "lev", pairs)
    return direct(True, own) + share


def solution(mesh):
    return jax.shard_map(
        local,
        mesh=mesh,
        in_specs=(
            P("lat", None, None, "lev"),
            P("lat", "lev", None),
            P("lat", None, None),
            P(),
            P(),
            P(),
        ),
        out_specs=P("lat", None, None, "lev"),
        check_vma=False,
    )
```

```python
import math

import jax
import jax.numpy as jnp
from jax import lax
from jax.experimental import pallas as pl
from jax.experimental.pallas import tpu as pltpu
from jax.sharding import PartitionSpec as P

BLK = 128
DEGREES = 2560
CHIPS = 16
F32 = jnp.float32
BF16 = jnp.bfloat16
VMEM = pl.BlockSpec(memory_space=pltpu.VMEM)
SMEM = pl.BlockSpec(memory_space=pltpu.SMEM)
NT = (((1,), (1,)), ((), ()))


def params(kib=16384):
    return pltpu.CompilerParams(vmem_limit_bytes=kib * 1024)


def wave_of(deal_ref, slot):
    deal = deal_ref[...]
    here = lax.broadcasted_iota(jnp.int32, deal.shape, 1) == slot
    return jnp.sum(jnp.where(here, deal, 0).astype(F32), axis=1, keepdims=True).astype(jnp.int32)


def live_degrees(wave, first_col, shape):
    degree = lax.broadcasted_iota(jnp.int32, shape, 0) + first_col
    return degree // BLK * BLK <= DEGREES - 1 - wave


def mask_rows(value, wave, degrees_live, row_block, row_blocks):
    rows_live = row_block >= wave * row_blocks // (2 * DEGREES)
    flags = jnp.logical_and(degrees_live, rows_live)
    return jnp.where(flags, value, jnp.zeros_like(value))


def inverse_kernel(deal_ref, spec_ref, own_ref, packed_ref, out_ref, other_ref):
    lat, lev = lax.axis_index("lat"), lax.axis_index("lev")
    core = lax.rem(lev, 2)
    slots, _, fields, cols = spec_ref.shape
    chips = out_ref.shape[0]
    fifths = out_ref.shape[1] // (16 * slots)
    mine = lev * cols
    theirs = (lev + 1 - 2 * core) * cols

    def stacked(pieces, first_col):
        column = lax.broadcasted_iota(jnp.int32, (fields, cols), 1) + first_col
        parity = (1 - 2 * lax.rem(column, 2)).astype(F32)
        rows = []
        for piece in pieces:
            rows.append(piece)
            rows.append((piece.astype(F32) * parity).astype(BF16))
        return jnp.concatenate(rows, axis=0)

    half_rows = fifths * 2 * BLK
    for slot in range(slots):
        wave = wave_of(deal_ref, slots * lat + slot)
        live = live_degrees(wave, theirs, (cols, BLK))
        left = stacked([spec_ref[slot, part] for part in range(2)], mine)
        other_left = stacked(
            [
                packed_ref[slot, part * fields : (part + 1) * fields, half_rows : half_rows + cols]
                for part in range(2)
            ],
            theirs,
        )
        for fifth in range(fifths):
            parts = []
            for half in range(2):
                begin = (2 * fifth + half) * BLK
                value = packed_ref[slot, :, begin : begin + BLK]
                row_block = 2 * fifths * core + 2 * fifth + half
                parts.append(mask_rows(value, wave, live, row_block, 4 * fifths))
            other_right = jnp.concatenate(parts, axis=1)
            here = slice(fifth * 2 * BLK, (fifth + 1) * 2 * BLK)
            other_ref[slot, :, here] = other_right
            value = jnp.dot(left, own_ref[slot, :, here], preferred_element_type=F32)
            value = value + jnp.dot(other_left, other_right, preferred_element_type=F32)
            start = (slot * fifths + fifth) * 16
            out_ref[:, start : start + 16, :] = value.T.astype(BF16).reshape(chips, 16, BLK)


def sum_kernel(in_ref, out_ref, spread):
    chips, rows, _ = in_ref.shape
    lats = out_ref.shape[0]
    groups = rows // 16
    fifths = groups // 2
    spread[...] = jnp.zeros_like(spread)
    for group in range(groups):
        piece = slice(group * 16, group * 16 + 16)
        total = in_ref[0, piece, :].astype(F32)
        for chip in range(1, chips):
            total = total + in_ref[chip, piece, :].astype(F32)
        slot, fifth = divmod(group, fifths)
        spread[pl.ds(slot * 8 + fifth, lats, stride=16), :] = total
    out_ref[...] = spread[...].astype(BF16).reshape(out_ref.shape)


def copies_kernel(in_ref, out_ref, spread):
    chips, rows, _ = out_ref.shape
    lats = in_ref.shape[0]
    groups = rows // 16
    fifths = groups // 2
    spread[...] = in_ref[...].astype(F32).reshape(spread.shape)
    for group in range(groups):
        slot, fifth = divmod(group, fifths)
        value = spread[pl.ds(slot * 8 + fifth, lats, stride=16), :].astype(BF16)
        for chip in range(chips):
            out_ref[chip, group * 16 : group * 16 + 16, :] = value


def circle(x, length):
    quarter = length * 0.25
    per = 1.0 / quarter
    turns = jnp.floor(x * per + 0.5)
    rest = x - turns * quarter
    more = jnp.floor(rest * per + 0.5)
    rest = rest - more * quarter
    turns = turns + more
    turns = turns - 4.0 * jnp.floor(turns * 0.25)
    angle = rest * ((2.0 * math.pi) / length)
    sq = angle * angle
    sine = angle * (
        1.0 + sq * (-1.0 / 6 + sq * (1.0 / 120 + sq * (-1.0 / 5040 + sq * (1.0 / 362880))))
    )
    cosine = 1.0 + sq * (
        -0.5 + sq * (1.0 / 24 + sq * (-1.0 / 720 + sq * (1.0 / 40320 + sq * (-1.0 / 3628800))))
    )
    odd = (turns == 1.0) | (turns == 3.0)
    first = jnp.where(odd, sine, cosine)
    second = jnp.where(odd, cosine, sine)
    first = jnp.where((turns == 1.0) | (turns == 2.0), -first, first)
    second = jnp.where(turns >= 2.0, -second, second)
    return first, second


def widths(core, fifths):
    return [2 * BLK * (core * fifths + fifth + 1) for fifth in range(fifths)]


def own_kernel(deal_ref, leg_ref, own_ref):
    lat, lev = lax.axis_index("lat"), lax.axis_index("lev")
    core = lax.rem(lev, 2)
    slots, cols, half_rows = own_ref.shape
    blocks = half_rows // BLK
    for slot in range(slots):
        wave = wave_of(deal_ref, slots * lat + slot)
        live = live_degrees(wave, lev * cols, (cols, BLK))
        for block in range(blocks):
            row_block = blocks * core + block
            value = leg_ref[slot, :, pl.ds(pl.multiple_of(row_block * BLK, BLK), BLK)]
            own_ref[slot, :, block * BLK : (block + 1) * BLK] = mask_rows(
                value, wave, live, row_block, 2 * blocks
            )


def table_kernel(fifths, deal_ref, lengths_ref, mixing_ref,
                 table_ref, turn_ref, weight_ref, mix_ref, gram_ref):
    lat, lev = lax.axis_index("lat"), lax.axis_index("lev")
    core = lax.rem(lev, 2)
    half_lat = lengths_ref.shape[0]
    half_rows = half_lat // 2
    waves = deal_ref.shape[0]
    fields = mixing_ref.shape[0]
    shape = (waves, BLK)
    sub = lax.broadcasted_iota(jnp.int32, shape, 0)
    lane = lax.broadcasted_iota(jnp.int32, shape, 1)
    lane_f = lane.astype(F32)
    wave = jnp.zeros(shape, jnp.int32)
    for slot in range(waves):
        wave = jnp.where(sub == slot, deal_ref[slot], wave)
    wave_f = wave.astype(F32)
    for pair in range(2):
        quarter = 2 * pair + (lane >= BLK // 2).astype(jnp.int32)
        turn = lax.rem(quarter * wave, 4)
        turn_ref[2 * pair] = jnp.where(turn == 0, 1.0, jnp.where(turn == 2, -1.0, 0.0))
        turn_ref[2 * pair + 1] = jnp.where(turn == 1, 1.0, jnp.where(turn == 3, -1.0, 0.0))
    size = mix_ref.shape[0]
    pick = (
        lax.rem(lax.broadcasted_iota(jnp.int32, (size, fields), 0), fields)
        == lax.broadcasted_iota(jnp.int32, (size, fields), 1)
    ).astype(F32).astype(BF16)
    tall = jnp.dot(pick, mixing_ref[...], preferred_element_type=F32).astype(BF16)
    wide = lax.dot_general(tall, pick, NT, preferred_element_type=F32)
    same = (
        lax.broadcasted_iota(jnp.int32, (size, size), 0) // fields
        == lax.broadcasted_iota(jnp.int32, (size, size), 1) // fields
    )
    mix_ref[...] = jnp.where(same, wide, 0.0).astype(BF16)
    weight_ref[...] = jnp.zeros_like(weight_ref)
    group = half_rows // fifths
    first_row = core * half_rows + (lev // 2) * (2 * BLK // CHIPS) + lat

    def build(which):
        main = widths(which, fifths)
        extra = sum(main)
        start = 0
        beyond = 0
        for fifth, width in enumerate(main):
            row = first_row + fifth * group
            length = lengths_ref[row]
            points = length // 4
            beyond = jnp.maximum(beyond, points - width)
            length_f = jnp.full(shape, length, jnp.int32).astype(F32)
            low_cos, low_sin = circle(wave_f * lane_f, length_f)
            high_cos, high_sin = circle(wave_f * lane_f * float(BLK), length_f)
            blocks = width // BLK
            for block in range(blocks + 1):
                a_cos = jnp.broadcast_to(high_cos[:, block : block + 1], shape)
                a_sin = jnp.broadcast_to(high_sin[:, block : block + 1], shape)
                cosine = a_cos * low_cos - a_sin * low_sin
                sine = a_sin * low_cos + a_cos * low_sin
                inside = lane + block * BLK < points
                begin = start + block * BLK if block < blocks else extra + fifth * BLK
                here = slice(begin, begin + BLK)
                table_ref[0:waves, here] = jnp.where(inside, cosine, 0.0).astype(BF16)
                table_ref[waves : 2 * waves, here] = jnp.where(inside, -sine, 0.0).astype(BF16)
            row_f = jnp.full((1, BLK), row, jnp.int32).astype(F32) + 0.5
            _, sine = circle(row_f, jnp.full((1, BLK), 4.0 * half_lat, F32))
            weight_ref[fifth : fifth + 1, :] = sine / jnp.sqrt(length_f[0:1, :])
            start += width
        weight_ref[fifths : fifths + 1, :] = jnp.full((1, BLK), beyond, jnp.int32).astype(F32)
        start = 0
        for fifth, width in enumerate(main):
            table = table_ref[:, start : start + width]
            gram = lax.dot_general(table, table, NT, preferred_element_type=F32)
            table = table_ref[:, extra + fifth * BLK : extra + (fifth + 1) * BLK]
            gram = gram + lax.dot_general(table, table, NT, preferred_element_type=F32)
            gram_ref[fifth] = two_terms(gram)
            start += width

    pl.when(core == 0)(lambda: build(0))
    pl.when(core == 1)(lambda: build(1))


def two_terms(value):
    high = value.astype(BF16)
    low = (value - high.astype(F32)).astype(BF16)
    return jnp.concatenate([high, low], axis=1)


def grid_kernel(scale, in_ref, table_ref, turn_ref, weight_ref, mix_ref, gram_ref,
                out_ref, spread, gathered, totals, mixed_coeffs):
    fifths = gram_ref.shape[0]
    waves = turn_ref.shape[1]
    core = lax.rem(lax.axis_index("lev"), 2)
    beyond = jnp.max(weight_ref[fifths : fifths + 1, :])
    lane = lax.broadcasted_iota(jnp.int32, (waves, BLK), 1)
    front = lane < BLK // 2
    spread[...] = in_ref[...].astype(F32).reshape(spread.shape)
    gathered[...] = jnp.zeros_like(gathered)
    mix = mix_ref[...]

    def analysed(table, fifth):
        twice = jnp.concatenate([table, table], axis=0)
        mixed = jnp.dot(mixed_coeffs[fifth], twice, preferred_element_type=F32)
        change = jnp.tanh(mixed).astype(BF16)
        return lax.dot_general(table, change, NT, preferred_element_type=F32)

    for fifth in range(fifths):
        value = spread[pl.ds(fifth, waves, stride=8), :] * scale
        swapped = pltpu.roll(value, BLK // 2, axis=1)
        real = jnp.where(front, value, swapped)
        imag = jnp.where(front, swapped, value)
        tops, bottoms = [], []
        for pair in range(2):
            cosine, sine = turn_ref[2 * pair], turn_ref[2 * pair + 1]
            tops.append(cosine * real - sine * imag)
            bottoms.append(sine * real + cosine * imag)
        coeffs = jnp.concatenate(
            [jnp.concatenate(tops, axis=1), jnp.concatenate(bottoms, axis=1)], axis=0
        ).astype(BF16)
        mixed_coeffs[fifth] = two_terms(
            lax.dot_general(mix, coeffs, NT, preferred_element_type=F32)
        )
        totals[fifth] = jnp.dot(
            gram_ref[fifth], jnp.concatenate([coeffs, coeffs], axis=0), preferred_element_type=F32
        )

    def rows(which):
        main = widths(which, fifths)
        start = 0
        for fifth, width in enumerate(main):
            total = totals[fifth]
            for begin in range(start, start + width, 4 * BLK):
                end = min(begin + 4 * BLK, start + width)
                total = total + analysed(table_ref[:, begin:end], fifth)
            totals[fifth] = total
            start += width
        @pl.when(beyond > 0.0)
        def _():
            for fifth in range(fifths):
                begin = start + fifth * BLK
                totals[fifth] += analysed(table_ref[:, begin : begin + BLK], fifth)

    pl.when(core == 0)(lambda: rows(0))
    pl.when(core == 1)(lambda: rows(1))

    for fifth in range(fifths):
        total = totals[fifth]
        real_sum = jnp.zeros((waves, BLK), F32)
        imag_sum = jnp.zeros((waves, BLK), F32)
        for pair in range(2):
            cosine, sine = turn_ref[2 * pair], turn_ref[2 * pair + 1]
            lanes = slice(pair * BLK, (pair + 1) * BLK)
            with_cos, with_sin = total[0:waves, lanes], total[waves : 2 * waves, lanes]
            real_sum = real_sum + cosine * with_cos + sine * with_sin
            imag_sum = imag_sum + cosine * with_sin - sine * with_cos
        real_sum = real_sum + pltpu.roll(real_sum, BLK // 2, axis=1)
        imag_sum = imag_sum + pltpu.roll(imag_sum, BLK // 2, axis=1)
        result = jnp.where(front, real_sum, imag_sum) * weight_ref[fifth : fifth + 1, :]
        gathered[pl.ds(fifth, waves, stride=8), :] = result
    out_ref[...] = gathered[...].astype(BF16).reshape(out_ref.shape)


def direct_kernel(mine, rows_ref, live_ref, out_ref):
    lev = lax.axis_index("lev")
    owner = lev if mine else lev + 1 - 2 * lax.rem(lev, 2)
    slots, cols, _ = live_ref.shape
    fields = out_ref.shape[2]
    chips, rows, _ = rows_ref.shape
    fifths = rows // (16 * slots)
    degree = lax.broadcasted_iota(jnp.int32, (cols, BLK), 0) + owner * cols
    parity = (1 - 2 * lax.rem(degree, 2)).astype(F32)
    for slot in range(slots):
        total = jnp.zeros((cols, BLK), F32)
        for fifth in range(fifths):
            start = (slot * fifths + fifth) * 16
            right = rows_ref[:, start : start + 16, :].reshape(chips * 16, BLK)
            left = live_ref[slot, :, fifth * 2 * BLK : (fifth + 1) * 2 * BLK]
            total = total + jnp.dot(left, right, preferred_element_type=F32)
        total = total + parity * pltpu.roll(total, BLK - fields, axis=1)
        turned = total.T
        for part in range(2):
            out_ref[slot, part] = turned[2 * part * fields : (2 * part + 1) * fields, :]


def local(spec_in, legendre, pattern, deal_list, circle_lengths, mixing):
    lats, levs = lax.axis_size("lat"), lax.axis_size("lev")
    chips = levs // 2
    slots, cols, half_lat = legendre.shape
    fields = spec_in.shape[2]
    waves = deal_list.shape[0]
    fifths = half_lat // (lats * levs)
    pairs = [(lev, lev ^ 1) for lev in range(levs)]
    same_core = [[2 * chip + core for chip in range(chips)] for core in range(2)]
    rows = slots * fifths * 16

    deal_row = deal_list.reshape(1, waves)
    half = half_lat // 2
    zero = jnp.zeros((), BF16)
    packed = jnp.where(
        lax.axis_index("lev") & 1 == 0,
        lax.pad(legendre, zero, ((0, 0, 0), (0, 0, 0), (-half, BLK, 0))),
        lax.pad(legendre, zero, ((0, 0, 0), (0, 0, 0), (0, BLK - half, 0))),
    )
    tail = jnp.pad(
        spec_in.reshape(slots, 2 * fields, cols),
        ((0, 0), (0, cols - 2 * fields), (half, BLK - cols)),
    )
    packed = jnp.where(lax.broadcasted_iota(jnp.int32, (1, 1, half + BLK), 2) < half, packed, tail)
    packed = lax.ppermute(packed, "lev", pairs)

    table, turns, weights, mix, grams = pl.pallas_call(
        lambda *refs: table_kernel(fifths, *refs),
        out_shape=(
            jax.ShapeDtypeStruct((2 * waves, sum(widths(1, fifths)) + fifths * BLK), BF16),
            jax.ShapeDtypeStruct((4, waves, BLK), F32),
            jax.ShapeDtypeStruct((8, BLK), F32),
            jax.ShapeDtypeStruct((8 * fields, 8 * fields), BF16),
            jax.ShapeDtypeStruct((fifths, 2 * waves, BLK), BF16),
        ),
        in_specs=[SMEM, SMEM, VMEM],
        out_specs=(VMEM,) * 5,
        compiler_params=params(),
        cost_estimate=pl.CostEstimate(flops=20_000_000, bytes_accessed=4_000_000, transcendentals=0),
        name="tables",
    )(deal_list, circle_lengths, mixing)
    own = pl.pallas_call(
        own_kernel,
        out_shape=jax.ShapeDtypeStruct((slots, cols, fifths * 2 * BLK), BF16),
        in_specs=[VMEM, VMEM],
        out_specs=VMEM,
        compiler_params=params(),
        cost_estimate=pl.CostEstimate(flops=1_000_000, bytes_accessed=1_300_000, transcendentals=0),
        name="own",
    )(deal_row, legendre)

    partial_sums, other = pl.pallas_call(
        inverse_kernel,
        out_shape=(
            jax.ShapeDtypeStruct((chips, rows, BLK), BF16),
            jax.ShapeDtypeStruct((slots, cols, fifths * 2 * BLK), BF16),
        ),
        in_specs=[VMEM] * 4,
        out_specs=(VMEM, VMEM),
        compiler_params=params(),
        name="inverse",
    )(deal_row, spec_in, own, packed)
    parts = lax.all_to_all(
        partial_sums, "lev", 0, 0, tiled=True, axis_index_groups=same_core
    )
    fourier = pl.pallas_call(
        sum_kernel,
        out_shape=jax.ShapeDtypeStruct((lats, 16, BLK), BF16),
        in_specs=[VMEM],
        out_specs=VMEM,
        scratch_shapes=[pltpu.VMEM((lats * 16, BLK), F32)],
        compiler_params=params(),
        name="sums",
    )(parts)
    fourier = lax.all_to_all(fourier, "lat", 0, 0, tiled=True)
    analysed = pl.pallas_call(
        lambda *refs: grid_kernel((2.0 * waves) ** (-0.5), *refs),
        out_shape=jax.ShapeDtypeStruct((lats, 16, BLK), BF16),
        in_specs=[VMEM] * 6,
        out_specs=VMEM,
        scratch_shapes=[
            pltpu.VMEM((lats * 16, BLK), F32),
            pltpu.VMEM((lats * 16, BLK), F32),
            pltpu.VMEM((fifths, 2 * waves, 8 * fields), F32),
            pltpu.VMEM((fifths, 8 * fields, BLK), BF16),
        ],
        compiler_params=params(24576),
        name="grid_rows",
    )(fourier, table, turns, weights, mix, grams)
    analysed = lax.all_to_all(analysed, "lat", 0, 0, tiled=True)
    copies = pl.pallas_call(
        copies_kernel,
        out_shape=jax.ShapeDtypeStruct((chips, rows, BLK), BF16),
        in_specs=[VMEM],
        out_specs=VMEM,
        scratch_shapes=[pltpu.VMEM((lats * 16, BLK), F32)],
        compiler_params=params(),
        name="copies",
    )(analysed)
    gathered = lax.all_to_all(copies, "lev", 0, 0, tiled=True, axis_index_groups=same_core)

    def direct(mine, live):
        return pl.pallas_call(
            lambda *refs: direct_kernel(mine, *refs),
            out_shape=jax.ShapeDtypeStruct((slots, 2, fields, cols), F32),
            in_specs=[VMEM, VMEM],
            out_specs=VMEM,
            compiler_params=params(),
            cost_estimate=pl.CostEstimate(
                flops=100_000_000, bytes_accessed=2_000_000, transcendentals=0
            ),
            name="direct_own" if mine else "direct_other",
        )(gathered, live)

    share = lax.ppermute(direct(False, other), "lev", pairs)
    return direct(True, own) + share


def solution(mesh):
    return jax.shard_map(
        local,
        mesh=mesh,
        in_specs=(
            P("lat", None, None, "lev"),
            P("lat", "lev", None),
            P("lat", None, None),
            P(),
            P(),
            P(),
        ),
        out_specs=P("lat", None, None, "lev"),
        check_vma=False,
    )
```

```python
import math

import jax
import jax.numpy as jnp
from jax import lax
from jax.experimental import pallas as pl
from jax.experimental.pallas import tpu as pltpu
from jax.sharding import PartitionSpec as P

BLK = 128
DEGREES = 2560
CHIPS = 16
F32 = jnp.float32
BF16 = jnp.bfloat16
VMEM = pl.BlockSpec(memory_space=pltpu.VMEM)
SMEM = pl.BlockSpec(memory_space=pltpu.SMEM)
NT = (((1,), (1,)), ((), ()))


def params(kib=16384):
    return pltpu.CompilerParams(vmem_limit_bytes=kib * 1024)


def wave_of(deal_ref, slot):
    deal = deal_ref[...]
    here = lax.broadcasted_iota(jnp.int32, deal.shape, 1) == slot
    return jnp.sum(jnp.where(here, deal, 0).astype(F32), axis=1, keepdims=True).astype(jnp.int32)


def live_degrees(wave, first_col, shape):
    degree = lax.broadcasted_iota(jnp.int32, shape, 0) + first_col
    return degree // BLK * BLK <= DEGREES - 1 - wave


def mask_rows(value, wave, degrees_live, row_block, row_blocks):
    rows_live = row_block >= wave * row_blocks // (2 * DEGREES)
    flags = jnp.logical_and(degrees_live, rows_live)
    return jnp.where(flags, value, jnp.zeros_like(value))


def inverse_kernel(deal_ref, spec_ref, own_ref, packed_ref, out_ref, other_ref):
    lat, lev = lax.axis_index("lat"), lax.axis_index("lev")
    core = lax.rem(lev, 2)
    slots, _, fields, cols = spec_ref.shape
    chips = out_ref.shape[0]
    fifths = out_ref.shape[1] // (16 * slots)
    mine = lev * cols
    theirs = (lev + 1 - 2 * core) * cols

    def stacked(pieces, first_col):
        column = lax.broadcasted_iota(jnp.int32, (fields, cols), 1) + first_col
        parity = (1 - 2 * lax.rem(column, 2)).astype(F32)
        rows = []
        for piece in pieces:
            rows.append(piece)
            rows.append((piece.astype(F32) * parity).astype(BF16))
        return jnp.concatenate(rows, axis=0)

    half_rows = fifths * 2 * BLK
    for slot in range(slots):
        wave = wave_of(deal_ref, slots * lat + slot)
        live = live_degrees(wave, theirs, (cols, BLK))
        left = stacked([spec_ref[slot, part] for part in range(2)], mine)
        other_left = stacked(
            [
                packed_ref[slot, part * fields : (part + 1) * fields, half_rows : half_rows + cols]
                for part in range(2)
            ],
            theirs,
        )
        for fifth in range(fifths):
            parts = []
            for half in range(2):
                begin = (2 * fifth + half) * BLK
                value = packed_ref[slot, :, begin : begin + BLK]
                row_block = 2 * fifths * core + 2 * fifth + half
                parts.append(mask_rows(value, wave, live, row_block, 4 * fifths))
            other_right = jnp.concatenate(parts, axis=1)
            here = slice(fifth * 2 * BLK, (fifth + 1) * 2 * BLK)
            other_ref[slot, :, here] = other_right
            value = jnp.dot(left, own_ref[slot, :, here], preferred_element_type=F32)
            value = value + jnp.dot(other_left, other_right, preferred_element_type=F32)
            start = (slot * fifths + fifth) * 16
            out_ref[:, start : start + 16, :] = value.T.astype(BF16).reshape(chips, 16, BLK)


def sum_kernel(in_ref, out_ref, spread):
    chips, rows, _ = in_ref.shape
    lats = out_ref.shape[0]
    groups = rows // 16
    fifths = groups // 2
    spread[...] = jnp.zeros_like(spread)
    for group in range(groups):
        piece = slice(group * 16, group * 16 + 16)
        total = in_ref[0, piece, :].astype(F32)
        for chip in range(1, chips):
            total = total + in_ref[chip, piece, :].astype(F32)
        slot, fifth = divmod(group, fifths)
        spread[pl.ds(slot * 8 + fifth, lats, stride=16), :] = total
    out_ref[...] = spread[...].astype(BF16).reshape(out_ref.shape)


def copies_kernel(in_ref, out_ref, spread):
    chips, rows, _ = out_ref.shape
    lats = in_ref.shape[0]
    groups = rows // 16
    fifths = groups // 2
    spread[...] = in_ref[...].astype(F32).reshape(spread.shape)
    for group in range(groups):
        slot, fifth = divmod(group, fifths)
        value = spread[pl.ds(slot * 8 + fifth, lats, stride=16), :].astype(BF16)
        for chip in range(chips):
            out_ref[chip, group * 16 : group * 16 + 16, :] = value


def circle(x, length):
    quarter = length * 0.25
    per = 1.0 / quarter
    turns = jnp.floor(x * per + 0.5)
    rest = x - turns * quarter
    more = jnp.floor(rest * per + 0.5)
    rest = rest - more * quarter
    turns = turns + more
    turns = turns - 4.0 * jnp.floor(turns * 0.25)
    angle = rest * ((2.0 * math.pi) / length)
    sq = angle * angle
    sine = angle * (
        1.0 + sq * (-1.0 / 6 + sq * (1.0 / 120 + sq * (-1.0 / 5040 + sq * (1.0 / 362880))))
    )
    cosine = 1.0 + sq * (
        -0.5 + sq * (1.0 / 24 + sq * (-1.0 / 720 + sq * (1.0 / 40320 + sq * (-1.0 / 3628800))))
    )
    odd = (turns == 1.0) | (turns == 3.0)
    first = jnp.where(odd, sine, cosine)
    second = jnp.where(odd, cosine, sine)
    first = jnp.where((turns == 1.0) | (turns == 2.0), -first, first)
    second = jnp.where(turns >= 2.0, -second, second)
    return first, second


def widths(core, fifths):
    return [2 * BLK * (core * fifths + fifth + 1) for fifth in range(fifths)]


def own_kernel(deal_ref, leg_ref, own_ref):
    lat, lev = lax.axis_index("lat"), lax.axis_index("lev")
    core = lax.rem(lev, 2)
    slots, cols, half_rows = own_ref.shape
    blocks = half_rows // BLK
    for slot in range(slots):
        wave = wave_of(deal_ref, slots * lat + slot)
        live = live_degrees(wave, lev * cols, (cols, BLK))
        for block in range(blocks):
            row_block = blocks * core + block
            value = leg_ref[slot, :, pl.ds(pl.multiple_of(row_block * BLK, BLK), BLK)]
            own_ref[slot, :, block * BLK : (block + 1) * BLK] = mask_rows(
                value, wave, live, row_block, 2 * blocks
            )


def table_kernel(fifths, deal_ref, lengths_ref, mixing_ref,
                 table_ref, turn_ref, weight_ref, mix_ref, gram_ref):
    lat, lev = lax.axis_index("lat"), lax.axis_index("lev")
    core = lax.rem(lev, 2)
    half_lat = lengths_ref.shape[0]
    half_rows = half_lat // 2
    waves = deal_ref.shape[0]
    fields = mixing_ref.shape[0]
    shape = (waves, BLK)
    sub = lax.broadcasted_iota(jnp.int32, shape, 0)
    lane = lax.broadcasted_iota(jnp.int32, shape, 1)
    lane_f = lane.astype(F32)
    wave = jnp.zeros(shape, jnp.int32)
    for slot in range(waves):
        wave = jnp.where(sub == slot, deal_ref[slot], wave)
    wave_f = wave.astype(F32)
    for pair in range(2):
        quarter = 2 * pair + (lane >= BLK // 2).astype(jnp.int32)
        turn = lax.rem(quarter * wave, 4)
        turn_ref[2 * pair] = jnp.where(turn == 0, 1.0, jnp.where(turn == 2, -1.0, 0.0))
        turn_ref[2 * pair + 1] = jnp.where(turn == 1, 1.0, jnp.where(turn == 3, -1.0, 0.0))
    size = mix_ref.shape[0]
    pick = (
        lax.rem(lax.broadcasted_iota(jnp.int32, (size, fields), 0), fields)
        == lax.broadcasted_iota(jnp.int32, (size, fields), 1)
    ).astype(F32).astype(BF16)
    tall = jnp.dot(pick, mixing_ref[...], preferred_element_type=F32).astype(BF16)
    wide = lax.dot_general(tall, pick, NT, preferred_element_type=F32)
    same = (
        lax.broadcasted_iota(jnp.int32, (size, size), 0) // fields
        == lax.broadcasted_iota(jnp.int32, (size, size), 1) // fields
    )
    mix_ref[...] = jnp.where(same, wide, 0.0).astype(BF16)
    weight_ref[...] = jnp.zeros_like(weight_ref)
    group = half_rows // fifths
    first_row = core * half_rows + (lev // 2) * (2 * BLK // CHIPS) + lat

    def build(which):
        main = widths(which, fifths)
        extra = sum(main)
        start = 0
        beyond = 0
        for fifth, width in enumerate(main):
            row = first_row + fifth * group
            length = lengths_ref[row]
            points = length // 4
            beyond = jnp.maximum(beyond, points - width)
            length_f = jnp.full(shape, length, jnp.int32).astype(F32)
            low_cos, low_sin = circle(wave_f * lane_f, length_f)
            high_cos, high_sin = circle(wave_f * lane_f * float(BLK), length_f)
            blocks = width // BLK
            for block in range(blocks + 1):
                a_cos = jnp.broadcast_to(high_cos[:, block : block + 1], shape)
                a_sin = jnp.broadcast_to(high_sin[:, block : block + 1], shape)
                cosine = a_cos * low_cos - a_sin * low_sin
                sine = a_sin * low_cos + a_cos * low_sin
                inside = lane + block * BLK < points
                begin = start + block * BLK if block < blocks else extra + fifth * BLK
                here = slice(begin, begin + BLK)
                table_ref[0:waves, here] = jnp.where(inside, cosine, 0.0).astype(BF16)
                table_ref[waves : 2 * waves, here] = jnp.where(inside, -sine, 0.0).astype(BF16)
            row_f = jnp.full((1, BLK), row, jnp.int32).astype(F32) + 0.5
            _, sine = circle(row_f, jnp.full((1, BLK), 4.0 * half_lat, F32))
            weight_ref[fifth : fifth + 1, :] = sine / jnp.sqrt(length_f[0:1, :])
            start += width
        weight_ref[fifths : fifths + 1, :] = jnp.full((1, BLK), beyond, jnp.int32).astype(F32)
        start = 0
        for fifth, width in enumerate(main):
            table = table_ref[:, start : start + width]
            gram = lax.dot_general(table, table, NT, preferred_element_type=F32)
            table = table_ref[:, extra + fifth * BLK : extra + (fifth + 1) * BLK]
            gram = gram + lax.dot_general(table, table, NT, preferred_element_type=F32)
            gram_ref[fifth] = two_terms(gram)
            start += width

    pl.when(core == 0)(lambda: build(0))
    pl.when(core == 1)(lambda: build(1))


def two_terms(value):
    high = value.astype(BF16)
    low = (value - high.astype(F32)).astype(BF16)
    return jnp.concatenate([high, low], axis=1)


def grid_kernel(scale, in_ref, table_ref, turn_ref, weight_ref, mix_ref, gram_ref,
                out_ref, spread, gathered, totals, mixed_coeffs):
    fifths = gram_ref.shape[0]
    waves = turn_ref.shape[1]
    core = lax.rem(lax.axis_index("lev"), 2)
    beyond = jnp.max(weight_ref[fifths : fifths + 1, :])
    lane = lax.broadcasted_iota(jnp.int32, (waves, BLK), 1)
    front = lane < BLK // 2
    spread[...] = in_ref[...].astype(F32).reshape(spread.shape)
    gathered[...] = jnp.zeros_like(gathered)
    mix = mix_ref[...]

    def analysed(table, fifth):
        twice = jnp.concatenate([table, table], axis=0)
        mixed = jnp.dot(mixed_coeffs[fifth], twice, preferred_element_type=F32)
        change = jnp.tanh(mixed).astype(BF16)
        return lax.dot_general(table, change, NT, preferred_element_type=F32)

    for fifth in range(fifths):
        value = spread[pl.ds(fifth, waves, stride=8), :] * scale
        swapped = pltpu.roll(value, BLK // 2, axis=1)
        real = jnp.where(front, value, swapped)
        imag = jnp.where(front, swapped, value)
        tops, bottoms = [], []
        for pair in range(2):
            cosine, sine = turn_ref[2 * pair], turn_ref[2 * pair + 1]
            tops.append(cosine * real - sine * imag)
            bottoms.append(sine * real + cosine * imag)
        coeffs = jnp.concatenate(
            [jnp.concatenate(tops, axis=1), jnp.concatenate(bottoms, axis=1)], axis=0
        ).astype(BF16)
        mixed_coeffs[fifth] = two_terms(
            lax.dot_general(mix, coeffs, NT, preferred_element_type=F32)
        )
        totals[fifth] = jnp.dot(
            gram_ref[fifth], jnp.concatenate([coeffs, coeffs], axis=0), preferred_element_type=F32
        )

    def rows(which):
        main = widths(which, fifths)
        start = 0
        for fifth, width in enumerate(main):
            total = totals[fifth]
            for begin in range(start, start + width, 4 * BLK):
                end = min(begin + 4 * BLK, start + width)
                total = total + analysed(table_ref[:, begin:end], fifth)
            totals[fifth] = total
            start += width
        @pl.when(beyond > 0.0)
        def _():
            for fifth in range(fifths):
                begin = start + fifth * BLK
                totals[fifth] += analysed(table_ref[:, begin : begin + BLK], fifth)

    pl.when(core == 0)(lambda: rows(0))
    pl.when(core == 1)(lambda: rows(1))

    for fifth in range(fifths):
        total = totals[fifth]
        real_sum = jnp.zeros((waves, BLK), F32)
        imag_sum = jnp.zeros((waves, BLK), F32)
        for pair in range(2):
            cosine, sine = turn_ref[2 * pair], turn_ref[2 * pair + 1]
            lanes = slice(pair * BLK, (pair + 1) * BLK)
            with_cos, with_sin = total[0:waves, lanes], total[waves : 2 * waves, lanes]
            real_sum = real_sum + cosine * with_cos + sine * with_sin
            imag_sum = imag_sum + cosine * with_sin - sine * with_cos
        real_sum = real_sum + pltpu.roll(real_sum, BLK // 2, axis=1)
        imag_sum = imag_sum + pltpu.roll(imag_sum, BLK // 2, axis=1)
        result = jnp.where(front, real_sum, imag_sum) * weight_ref[fifth : fifth + 1, :]
        gathered[pl.ds(fifth, waves, stride=8), :] = result
    out_ref[...] = gathered[...].astype(BF16).reshape(out_ref.shape)


def direct_kernel(mine, rows_ref, live_ref, out_ref):
    lev = lax.axis_index("lev")
    owner = lev if mine else lev + 1 - 2 * lax.rem(lev, 2)
    slots, cols, _ = live_ref.shape
    fields = out_ref.shape[2]
    chips, rows, _ = rows_ref.shape
    fifths = rows // (16 * slots)
    degree = lax.broadcasted_iota(jnp.int32, (cols, BLK), 0) + owner * cols
    parity = (1 - 2 * lax.rem(degree, 2)).astype(F32)
    for slot in range(slots):
        total = jnp.zeros((cols, BLK), F32)
        for fifth in range(fifths):
            start = (slot * fifths + fifth) * 16
            right = rows_ref[:, start : start + 16, :].reshape(chips * 16, BLK)
            left = live_ref[slot, :, fifth * 2 * BLK : (fifth + 1) * 2 * BLK]
            total = total + jnp.dot(left, right, preferred_element_type=F32)
        total = total + parity * pltpu.roll(total, BLK - fields, axis=1)
        turned = total.T
        for part in range(2):
            out_ref[slot, part] = turned[2 * part * fields : (2 * part + 1) * fields, :]


def local(spec_in, legendre, pattern, deal_list, circle_lengths, mixing):
    lats, levs = lax.axis_size("lat"), lax.axis_size("lev")
    chips = levs // 2
    slots, cols, half_lat = legendre.shape
    fields = spec_in.shape[2]
    waves = deal_list.shape[0]
    fifths = half_lat // (lats * levs)
    pairs = [(lev, lev ^ 1) for lev in range(levs)]
    same_core = [[2 * chip + core for chip in range(chips)] for core in range(2)]
    rows = slots * fifths * 16

    deal_row = deal_list.reshape(1, waves)
    half = half_lat // 2
    zero = jnp.zeros((), BF16)
    packed = lax.dynamic_slice(
        lax.pad(legendre, zero, ((0, 0, 0), (0, 0, 0), (0, BLK, 0))),
        (0, 0, half * (1 - (lax.axis_index("lev") & 1))),
        (slots, cols, half + BLK),
    )
    tail = jnp.pad(
        spec_in.reshape(slots, 2 * fields, cols),
        ((0, 0), (0, cols - 2 * fields), (half, BLK - cols)),
    )
    packed = jnp.where(lax.broadcasted_iota(jnp.int32, (1, 1, half + BLK), 2) < half, packed, tail)
    packed = lax.ppermute(packed, "lev", pairs)

    table, turns, weights, mix, grams = pl.pallas_call(
        lambda *refs: table_kernel(fifths, *refs),
        out_shape=(
            jax.ShapeDtypeStruct((2 * waves, sum(widths(1, fifths)) + fifths * BLK), BF16),
            jax.ShapeDtypeStruct((4, waves, BLK), F32),
            jax.ShapeDtypeStruct((8, BLK), F32),
            jax.ShapeDtypeStruct((8 * fields, 8 * fields), BF16),
            jax.ShapeDtypeStruct((fifths, 2 * waves, BLK), BF16),
        ),
        in_specs=[SMEM, SMEM, VMEM],
        out_specs=(VMEM,) * 5,
        compiler_params=params(),
        cost_estimate=pl.CostEstimate(flops=20_000_000, bytes_accessed=4_000_000, transcendentals=0),
        name="tables",
    )(deal_list, circle_lengths, mixing)
    own = pl.pallas_call(
        own_kernel,
        out_shape=jax.ShapeDtypeStruct((slots, cols, fifths * 2 * BLK), BF16),
        in_specs=[VMEM, VMEM],
        out_specs=VMEM,
        compiler_params=params(),
        cost_estimate=pl.CostEstimate(flops=1_000_000, bytes_accessed=1_300_000, transcendentals=0),
        name="own",
    )(deal_row, legendre)

    partial_sums, other = pl.pallas_call(
        inverse_kernel,
        out_shape=(
            jax.ShapeDtypeStruct((chips, rows, BLK), BF16),
            jax.ShapeDtypeStruct((slots, cols, fifths * 2 * BLK), BF16),
        ),
        in_specs=[VMEM] * 4,
        out_specs=(VMEM, VMEM),
        compiler_params=params(),
        name="inverse",
    )(deal_row, spec_in, own, packed)
    parts = lax.all_to_all(
        partial_sums, "lev", 0, 0, tiled=True, axis_index_groups=same_core
    )
    fourier = pl.pallas_call(
        sum_kernel,
        out_shape=jax.ShapeDtypeStruct((lats, 16, BLK), BF16),
        in_specs=[VMEM],
        out_specs=VMEM,
        scratch_shapes=[pltpu.VMEM((lats * 16, BLK), F32)],
        compiler_params=params(),
        name="sums",
    )(parts)
    fourier = lax.all_to_all(fourier, "lat", 0, 0, tiled=True)
    analysed = pl.pallas_call(
        lambda *refs: grid_kernel((2.0 * waves) ** (-0.5), *refs),
        out_shape=jax.ShapeDtypeStruct((lats, 16, BLK), BF16),
        in_specs=[VMEM] * 6,
        out_specs=VMEM,
        scratch_shapes=[
            pltpu.VMEM((lats * 16, BLK), F32),
            pltpu.VMEM((lats * 16, BLK), F32),
            pltpu.VMEM((fifths, 2 * waves, 8 * fields), F32),
            pltpu.VMEM((fifths, 8 * fields, BLK), BF16),
        ],
        compiler_params=params(24576),
        name="grid_rows",
    )(fourier, table, turns, weights, mix, grams)
    analysed = lax.all_to_all(analysed, "lat", 0, 0, tiled=True)
    copies = pl.pallas_call(
        copies_kernel,
        out_shape=jax.ShapeDtypeStruct((chips, rows, BLK), BF16),
        in_specs=[VMEM],
        out_specs=VMEM,
        scratch_shapes=[pltpu.VMEM((lats * 16, BLK), F32)],
        compiler_params=params(),
        name="copies",
    )(analysed)
    gathered = lax.all_to_all(copies, "lev", 0, 0, tiled=True, axis_index_groups=same_core)

    def direct(mine, live):
        return pl.pallas_call(
            lambda *refs: direct_kernel(mine, *refs),
            out_shape=jax.ShapeDtypeStruct((slots, 2, fields, cols), F32),
            in_specs=[VMEM, VMEM],
            out_specs=VMEM,
            compiler_params=params(),
            cost_estimate=pl.CostEstimate(
                flops=100_000_000, bytes_accessed=2_000_000, transcendentals=0
            ),
            name="direct_own" if mine else "direct_other",
        )(gathered, live)

    share = lax.ppermute(direct(False, other), "lev", pairs)
    return direct(True, own) + share


def solution(mesh):
    return jax.shard_map(
        local,
        mesh=mesh,
        in_specs=(
            P("lat", None, None, "lev"),
            P("lat", "lev", None),
            P("lat", None, None),
            P(),
            P(),
            P(),
        ),
        out_specs=P("lat", None, None, "lev"),
        check_vma=False,
    )
```

```python
import math

import jax
import jax.numpy as jnp
from jax import lax
from jax.experimental import pallas as pl
from jax.experimental.pallas import tpu as pltpu
from jax.sharding import PartitionSpec as P

BLK = 128
DEGREES = 2560
CHIPS = 16
F32 = jnp.float32
BF16 = jnp.bfloat16
VMEM = pl.BlockSpec(memory_space=pltpu.VMEM)
NT = (((1,), (1,)), ((), ()))


def params(kib=16384):
    return pltpu.CompilerParams(vmem_limit_bytes=kib * 1024)


def rows_block(core, fifth, fifths):
    if fifth == fifths - 1:
        return 2 * fifths - 1 - core
    return core * (fifths - 1) + fifth


def wave_of(deal_ref, slot):
    deal = deal_ref[...]
    here = lax.broadcasted_iota(jnp.int32, deal.shape, 1) == slot
    return jnp.sum(jnp.where(here, deal, 0).astype(F32), axis=1, keepdims=True).astype(jnp.int32)


def live_degrees(wave, first_col, shape):
    degree = lax.broadcasted_iota(jnp.int32, shape, 0) + first_col
    return degree // BLK * BLK <= DEGREES - 1 - wave


def mask_rows(value, wave, degrees_live, row_block, row_blocks):
    rows_live = row_block >= wave * row_blocks // (2 * DEGREES)
    flags = jnp.logical_and(degrees_live, rows_live)
    return jnp.where(flags, value, jnp.zeros_like(value))


def inverse_kernel(deal_ref, spec_ref, own_ref, packed_ref, out_ref, other_ref):
    lat, lev = lax.axis_index("lat"), lax.axis_index("lev")
    core = lax.rem(lev, 2)
    slots, _, fields, cols = spec_ref.shape
    chips = out_ref.shape[0]
    fifths = out_ref.shape[1] // (16 * slots)
    mine = lev * cols
    theirs = (lev + 1 - 2 * core) * cols

    def stacked(pieces, first_col):
        column = lax.broadcasted_iota(jnp.int32, (fields, cols), 1) + first_col
        parity = (1 - 2 * lax.rem(column, 2)).astype(F32)
        rows = []
        for piece in pieces:
            rows.append(piece)
            rows.append((piece.astype(F32) * parity).astype(BF16))
        return jnp.concatenate(rows, axis=0)

    half_rows = fifths * 2 * BLK
    for slot in range(slots):
        wave = wave_of(deal_ref, slots * lat + slot)
        live = live_degrees(wave, theirs, (cols, BLK))
        left = stacked([spec_ref[slot, part] for part in range(2)], mine)
        other_left = stacked(
            [
                packed_ref[slot, part * fields : (part + 1) * fields, half_rows : half_rows + cols]
                for part in range(2)
            ],
            theirs,
        )
        for fifth in range(fifths):
            parts = []
            for half in range(2):
                begin = (2 * fifth + half) * BLK
                value = packed_ref[slot, :, begin : begin + BLK]
                row_block = 2 * rows_block(core, fifth, fifths) + half
                parts.append(mask_rows(value, wave, live, row_block, 4 * fifths))
            other_right = jnp.concatenate(parts, axis=1)
            here = slice(fifth * 2 * BLK, (fifth + 1) * 2 * BLK)
            other_ref[slot, :, here] = other_right
            value = jnp.dot(left, own_ref[slot, :, here], preferred_element_type=F32)
            value = value + jnp.dot(other_left, other_right, preferred_element_type=F32)
            start = (slot * fifths + fifth) * 16
            out_ref[:, start : start + 16, :] = value.T.astype(BF16).reshape(chips, 16, BLK)


def sum_kernel(in_ref, out_ref, spread):
    chips, rows, _ = in_ref.shape
    lats = out_ref.shape[0]
    groups = rows // 16
    fifths = groups // 2
    spread[...] = jnp.zeros_like(spread)
    for group in range(groups):
        piece = slice(group * 16, group * 16 + 16)
        total = in_ref[0, piece, :].astype(F32)
        for chip in range(1, chips):
            total = total + in_ref[chip, piece, :].astype(F32)
        slot, fifth = divmod(group, fifths)
        spread[pl.ds(slot * 8 + fifth, lats, stride=16), :] = total
    out_ref[...] = spread[...].astype(BF16).reshape(out_ref.shape)


def copies_kernel(in_ref, out_ref, spread):
    chips, rows, _ = out_ref.shape
    lats = in_ref.shape[0]
    groups = rows // 16
    fifths = groups // 2
    spread[...] = in_ref[...].astype(F32).reshape(spread.shape)
    for group in range(groups):
        slot, fifth = divmod(group, fifths)
        value = spread[pl.ds(slot * 8 + fifth, lats, stride=16), :].astype(BF16)
        for chip in range(chips):
            out_ref[chip, group * 16 : group * 16 + 16, :] = value


def circle(x, length):
    quarter = length * 0.25
    per = 1.0 / quarter
    turns = jnp.floor(x * per + 0.5)
    rest = x - turns * quarter
    more = jnp.floor(rest * per + 0.5)
    rest = rest - more * quarter
    turns = turns + more
    turns = turns - 4.0 * jnp.floor(turns * 0.25)
    angle = rest * ((2.0 * math.pi) / length)
    sq = angle * angle
    sine = angle * (
        1.0 + sq * (-1.0 / 6 + sq * (1.0 / 120 + sq * (-1.0 / 5040 + sq * (1.0 / 362880))))
    )
    cosine = 1.0 + sq * (
        -0.5 + sq * (1.0 / 24 + sq * (-1.0 / 720 + sq * (1.0 / 40320 + sq * (-1.0 / 3628800))))
    )
    odd = (turns == 1.0) | (turns == 3.0)
    first = jnp.where(odd, sine, cosine)
    second = jnp.where(odd, cosine, sine)
    first = jnp.where((turns == 1.0) | (turns == 2.0), -first, first)
    second = jnp.where(turns >= 2.0, -second, second)
    return first, second


def widths(core, fifths):
    return [2 * BLK * (rows_block(core, fifth, fifths) + 1) for fifth in range(fifths)]


def own_rows(deal_ref, leg_ref, own_ref):
    lat, lev = lax.axis_index("lat"), lax.axis_index("lev")
    core = lax.rem(lev, 2)
    slots, cols, half_rows = own_ref.shape
    blocks = half_rows // BLK
    fifths = blocks // 2
    for slot in range(slots):
        wave = wave_of(deal_ref, slots * lat + slot)
        live = live_degrees(wave, lev * cols, (cols, BLK))
        for block in range(blocks):
            row_block = 2 * rows_block(core, block // 2, fifths) + block % 2
            value = leg_ref[slot, :, pl.ds(pl.multiple_of(row_block * BLK, BLK), BLK)]
            own_ref[slot, :, block * BLK : (block + 1) * BLK] = mask_rows(
                value, wave, live, row_block, 2 * blocks
            )


def table_kernel(fifths, deal_ref, lengths_ref, mixing_ref, leg_ref,
                 own_ref, table_ref, turn_ref, weight_ref, mix_ref, gram_ref):
    lat, lev = lax.axis_index("lat"), lax.axis_index("lev")
    core = lax.rem(lev, 2)
    half_lat = lengths_ref.shape[0] * BLK
    half_rows = half_lat // 2
    waves = deal_ref.shape[1]
    own_rows(deal_ref, leg_ref, own_ref)
    fields = mixing_ref.shape[0]
    shape = (waves, BLK)
    sub = lax.broadcasted_iota(jnp.int32, shape, 0)
    lane = lax.broadcasted_iota(jnp.int32, shape, 1)
    lane_f = lane.astype(F32)
    square = (waves, waves)
    diagonal = lax.broadcasted_iota(jnp.int32, square, 0) == lax.broadcasted_iota(jnp.int32, square, 1)
    wave_f = jnp.where(diagonal, jnp.broadcast_to(deal_ref[...], square), 0).astype(F32)
    wave_f = jnp.broadcast_to(jnp.sum(wave_f, axis=1, keepdims=True), shape)
    wave = wave_f.astype(jnp.int32)
    lengths = lengths_ref[...]
    position = lax.broadcasted_iota(jnp.int32, lengths.shape, 0) * BLK
    position = position + lax.broadcasted_iota(jnp.int32, lengths.shape, 1)
    for pair in range(2):
        quarter = 2 * pair + (lane >= BLK // 2).astype(jnp.int32)
        turn = lax.rem(quarter * wave, 4)
        turn_ref[2 * pair] = jnp.where(turn == 0, 1.0, jnp.where(turn == 2, -1.0, 0.0))
        turn_ref[2 * pair + 1] = jnp.where(turn == 1, 1.0, jnp.where(turn == 3, -1.0, 0.0))
    size = mix_ref.shape[0]
    pick = (
        lax.rem(lax.broadcasted_iota(jnp.int32, (size, fields), 0), fields)
        == lax.broadcasted_iota(jnp.int32, (size, fields), 1)
    ).astype(F32).astype(BF16)
    tall = jnp.dot(pick, mixing_ref[...], preferred_element_type=F32).astype(BF16)
    wide = lax.dot_general(tall, pick, NT, preferred_element_type=F32)
    same = (
        lax.broadcasted_iota(jnp.int32, (size, size), 0) // fields
        == lax.broadcasted_iota(jnp.int32, (size, size), 1) // fields
    )
    mix_ref[...] = jnp.where(same, wide, 0.0).astype(BF16)
    weight_ref[...] = jnp.zeros_like(weight_ref)
    group = half_rows // fifths
    first_row = (lev // 2) * (group // CHIPS) + lat

    def build(which):
        main = widths(which, fifths)
        extra = sum(main)
        start = 0
        beyond = jnp.zeros((1, 1), F32)
        for fifth, width in enumerate(main):
            row = first_row + rows_block(which, fifth, fifths) * group
            length_f = jnp.where(position == row, lengths, 0).astype(F32)
            length_f = jnp.sum(jnp.sum(length_f, axis=0, keepdims=True), axis=1, keepdims=True)
            beyond = jnp.maximum(beyond, length_f * 0.25 - float(width))
            length_f = jnp.broadcast_to(length_f, shape)
            points = length_f * 0.25
            low_cos, low_sin = circle(wave_f * lane_f, length_f)
            high_cos, high_sin = circle(wave_f * lane_f * float(BLK), length_f)
            blocks = width // BLK
            for block in range(blocks + 1):
                a_cos = jnp.broadcast_to(high_cos[:, block : block + 1], shape)
                a_sin = jnp.broadcast_to(high_sin[:, block : block + 1], shape)
                cosine = a_cos * low_cos - a_sin * low_sin
                sine = a_sin * low_cos + a_cos * low_sin
                inside = lane_f + float(block * BLK) < points
                begin = start + block * BLK if block < blocks else extra + fifth * BLK
                here = slice(begin, begin + BLK)
                if block >= rows_block(which, fifth, fifths):
                    cosine = jnp.where(inside, cosine, 0.0)
                    sine = jnp.where(inside, sine, 0.0)
                table_ref[0:waves, here] = cosine.astype(BF16)
                table_ref[waves : 2 * waves, here] = (-sine).astype(BF16)
            row_f = jnp.full((1, BLK), row, jnp.int32).astype(F32) + 0.5
            _, sine = circle(row_f, jnp.full((1, BLK), 4.0 * half_lat, F32))
            weight_ref[fifth : fifth + 1, :] = sine / jnp.sqrt(length_f[0:1, :])
            start += width
        weight_ref[fifths : fifths + 1, :] = jnp.broadcast_to(beyond, (1, BLK))
        start = 0
        for fifth, width in enumerate(main):
            table = table_ref[:, start : start + width]
            gram = lax.dot_general(table, table, NT, preferred_element_type=F32)
            table = table_ref[:, extra + fifth * BLK : extra + (fifth + 1) * BLK]
            gram = gram + lax.dot_general(table, table, NT, preferred_element_type=F32)
            gram_ref[fifth] = two_terms(gram)
            start += width

    pl.when(core == 0)(lambda: build(0))
    pl.when(core == 1)(lambda: build(1))


def two_terms(value):
    high = value.astype(BF16)
    low = (value - high.astype(F32)).astype(BF16)
    return jnp.concatenate([high, low], axis=1)


def grid_kernel(scale, in_ref, table_ref, turn_ref, weight_ref, mix_ref, gram_ref,
                out_ref, spread, gathered, totals, mixed_coeffs):
    fifths = gram_ref.shape[0]
    waves = turn_ref.shape[1]
    core = lax.rem(lax.axis_index("lev"), 2)
    beyond = jnp.max(weight_ref[fifths : fifths + 1, :])
    lane = lax.broadcasted_iota(jnp.int32, (waves, BLK), 1)
    front = lane < BLK // 2
    spread[...] = in_ref[...].astype(F32).reshape(spread.shape)
    gathered[...] = jnp.zeros_like(gathered)
    mix = mix_ref[...]

    def analysed(table, fifth):
        twice = jnp.concatenate([table, table], axis=0)
        mixed = jnp.dot(mixed_coeffs[fifth], twice, preferred_element_type=F32)
        change = jnp.tanh(mixed).astype(BF16)
        return lax.dot_general(table, change, NT, preferred_element_type=F32)

    for fifth in range(fifths):
        value = spread[pl.ds(fifth, waves, stride=8), :] * scale
        swapped = pltpu.roll(value, BLK // 2, axis=1)
        real = jnp.where(front, value, swapped)
        imag = jnp.where(front, swapped, value)
        tops, bottoms = [], []
        for pair in range(2):
            cosine, sine = turn_ref[2 * pair], turn_ref[2 * pair + 1]
            tops.append(cosine * real - sine * imag)
            bottoms.append(sine * real + cosine * imag)
        coeffs = jnp.concatenate(
            [jnp.concatenate(tops, axis=1), jnp.concatenate(bottoms, axis=1)], axis=0
        ).astype(BF16)
        mixed_coeffs[fifth] = two_terms(
            lax.dot_general(mix, coeffs, NT, preferred_element_type=F32)
        )
        totals[fifth] = jnp.dot(
            gram_ref[fifth], jnp.concatenate([coeffs, coeffs], axis=0), preferred_element_type=F32
        )

    def rows(which):
        main = widths(which, fifths)
        start = 0
        for fifth, width in enumerate(main):
            total = totals[fifth]
            for begin in range(start, start + width, 4 * BLK):
                end = min(begin + 4 * BLK, start + width)
                total = total + analysed(table_ref[:, begin:end], fifth)
            totals[fifth] = total
            start += width
        @pl.when(beyond > 0.0)
        def _():
            for fifth in range(fifths):
                begin = start + fifth * BLK
                totals[fifth] += analysed(table_ref[:, begin : begin + BLK], fifth)

    pl.when(core == 0)(lambda: rows(0))
    pl.when(core == 1)(lambda: rows(1))

    for fifth in range(fifths):
        total = totals[fifth]
        real_sum = jnp.zeros((waves, BLK), F32)
        imag_sum = jnp.zeros((waves, BLK), F32)
        for pair in range(2):
            cosine, sine = turn_ref[2 * pair], turn_ref[2 * pair + 1]
            lanes = slice(pair * BLK, (pair + 1) * BLK)
            with_cos, with_sin = total[0:waves, lanes], total[waves : 2 * waves, lanes]
            real_sum = real_sum + cosine * with_cos + sine * with_sin
            imag_sum = imag_sum + cosine * with_sin - sine * with_cos
        real_sum = real_sum + pltpu.roll(real_sum, BLK // 2, axis=1)
        imag_sum = imag_sum + pltpu.roll(imag_sum, BLK // 2, axis=1)
        result = jnp.where(front, real_sum, imag_sum) * weight_ref[fifth : fifth + 1, :]
        gathered[pl.ds(fifth, waves, stride=8), :] = result
    out_ref[...] = gathered[...].astype(BF16).reshape(out_ref.shape)


def direct_kernel(mine, rows_ref, live_ref, out_ref):
    lev = lax.axis_index("lev")
    owner = lev if mine else lev + 1 - 2 * lax.rem(lev, 2)
    slots, cols, _ = live_ref.shape
    fields = out_ref.shape[2]
    chips, rows, _ = rows_ref.shape
    fifths = rows // (16 * slots)
    degree = lax.broadcasted_iota(jnp.int32, (cols, BLK), 0) + owner * cols
    parity = (1 - 2 * lax.rem(degree, 2)).astype(F32)
    for slot in range(slots):
        total = jnp.zeros((cols, BLK), F32)
        for fifth in range(fifths):
            start = (slot * fifths + fifth) * 16
            right = rows_ref[:, start : start + 16, :].reshape(chips * 16, BLK)
            left = live_ref[slot, :, fifth * 2 * BLK : (fifth + 1) * 2 * BLK]
            total = total + jnp.dot(left, right, preferred_element_type=F32)
        total = total + parity * pltpu.roll(total, BLK - fields, axis=1)
        turned = total.T
        for part in range(2):
            out_ref[slot, part] = turned[2 * part * fields : (2 * part + 1) * fields, :]


def local(spec_in, legendre, pattern, deal_list, circle_lengths, mixing):
    lats, levs = lax.axis_size("lat"), lax.axis_size("lev")
    chips = levs // 2
    slots, cols, half_lat = legendre.shape
    fields = spec_in.shape[2]
    waves = deal_list.shape[0]
    fifths = half_lat // (lats * levs)
    pairs = [(lev, lev ^ 1) for lev in range(levs)]
    same_core = [[2 * chip + core for chip in range(chips)] for core in range(2)]
    rows = slots * fifths * 16

    deal_row = deal_list.reshape(1, waves)
    half = half_lat // 2
    other_core = 1 - (lax.axis_index("lev") & 1)
    zero = jnp.zeros((), BF16)
    group = half // fifths
    first = half - group
    padded = lax.pad(legendre, zero, ((0, 0, 0), (0, 0, 0), (0, half, 0)))
    size = (slots, cols, half + BLK)
    lanes = lax.broadcasted_iota(jnp.int32, (1, 1, half + BLK), 2)
    tail = jnp.pad(
        spec_in.reshape(slots, 2 * fields, cols),
        ((0, 0), (0, cols - 2 * fields), (half, BLK - cols)),
    )
    packed = jnp.where(
        lanes < half,
        jnp.where(
            lanes < first,
            lax.dynamic_slice(padded, (0, 0, first * other_core), size),
            lax.dynamic_slice(padded, (0, 0, half_lat - half - group * other_core), size),
        ),
        tail,
    )
    packed = lax.ppermute(packed, "lev", pairs)

    own, table, turns, weights, mix, grams = pl.pallas_call(
        lambda *refs: table_kernel(fifths, *refs),
        out_shape=(
            jax.ShapeDtypeStruct((slots, cols, fifths * 2 * BLK), BF16),
            jax.ShapeDtypeStruct((2 * waves, sum(widths(1, fifths)) + fifths * BLK), BF16),
            jax.ShapeDtypeStruct((4, waves, BLK), F32),
            jax.ShapeDtypeStruct((8, BLK), F32),
            jax.ShapeDtypeStruct((8 * fields, 8 * fields), BF16),
            jax.ShapeDtypeStruct((fifths, 2 * waves, BLK), BF16),
        ),
        in_specs=[VMEM] * 4,
        out_specs=(VMEM,) * 6,
        compiler_params=params(),
        cost_estimate=pl.CostEstimate(flops=20_000_000, bytes_accessed=4_000_000, transcendentals=0),
        name="tables",
    )(deal_row, circle_lengths.reshape(-1, BLK), mixing, legendre)

    partial_sums, other = pl.pallas_call(
        inverse_kernel,
        out_shape=(
            jax.ShapeDtypeStruct((chips, rows, BLK), BF16),
            jax.ShapeDtypeStruct((slots, cols, fifths * 2 * BLK), BF16),
        ),
        in_specs=[VMEM] * 4,
        out_specs=(VMEM, VMEM),
        compiler_params=params(),
        name="inverse",
    )(deal_row, spec_in, own, packed)
    parts = lax.all_to_all(
        partial_sums, "lev", 0, 0, tiled=True, axis_index_groups=same_core
    )
    fourier = pl.pallas_call(
        sum_kernel,
        out_shape=jax.ShapeDtypeStruct((lats, 16, BLK), BF16),
        in_specs=[VMEM],
        out_specs=VMEM,
        scratch_shapes=[pltpu.VMEM((lats * 16, BLK), F32)],
        compiler_params=params(),
        name="sums",
    )(parts)
    fourier = lax.all_to_all(fourier, "lat", 0, 0, tiled=True)
    analysed = pl.pallas_call(
        lambda *refs: grid_kernel((2.0 * waves) ** (-0.5), *refs),
        out_shape=jax.ShapeDtypeStruct((lats, 16, BLK), BF16),
        in_specs=[VMEM] * 6,
        out_specs=VMEM,
        scratch_shapes=[
            pltpu.VMEM((lats * 16, BLK), F32),
            pltpu.VMEM((lats * 16, BLK), F32),
            pltpu.VMEM((fifths, 2 * waves, 8 * fields), F32),
            pltpu.VMEM((fifths, 8 * fields, BLK), BF16),
        ],
        compiler_params=params(24576),
        name="grid_rows",
    )(fourier, table, turns, weights, mix, grams)
    analysed = lax.all_to_all(analysed, "lat", 0, 0, tiled=True)
    copies = pl.pallas_call(
        copies_kernel,
        out_shape=jax.ShapeDtypeStruct((chips, rows, BLK), BF16),
        in_specs=[VMEM],
        out_specs=VMEM,
        scratch_shapes=[pltpu.VMEM((lats * 16, BLK), F32)],
        compiler_params=params(),
        name="copies",
    )(analysed)
    gathered = lax.all_to_all(copies, "lev", 0, 0, tiled=True, axis_index_groups=same_core)

    def direct(mine, live):
        return pl.pallas_call(
            lambda *refs: direct_kernel(mine, *refs),
            out_shape=jax.ShapeDtypeStruct((slots, 2, fields, cols), F32),
            in_specs=[VMEM, VMEM],
            out_specs=VMEM,
            compiler_params=params(),
            cost_estimate=pl.CostEstimate(
                flops=100_000_000, bytes_accessed=2_000_000, transcendentals=0
            ),
            name="direct_own" if mine else "direct_other",
        )(gathered, live)

    share = lax.ppermute(direct(False, other), "lev", pairs)
    return direct(True, own) + share


def solution(mesh):
    return jax.shard_map(
        local,
        mesh=mesh,
        in_specs=(
            P("lat", None, None, "lev"),
            P("lat", "lev", None),
            P("lat", None, None),
            P(),
            P(),
            P(),
        ),
        out_specs=P("lat", None, None, "lev"),
        check_vma=False,
    )
```
